1024 devices in a mesh: gx: 32 (over z, core), gy: 32 (over x, y).
Axes of the slice: x: 4, y: 8, z: 16, core: 2. Of those that a mesh axis runs over, the one named last changes fastest.
Arguments:
- vorticity: float32 [38, 4096, 4096], P(None, 'gx', 'gy'), may hold values from 0.05 to 20
Outputs:
- leaders_fine: float32 [36, 2048, 2048], P(None, 'gx', 'gy')
- leaders_middle: float32 [36, 1024, 1024], P(None, 'gx', 'gy')
- leaders_coarse: float32 [36, 512, 512], P(None, 'gx', 'gy')
The draws below stay inside these ranges and needn't reach their ends.
All inputs are finite; a program needn't handle non-finite values.
Results may differ from the reference program's by a relative error of at most 0.000082.
Values sent between devices are 32-bit elements; how exact they have to be, the bound alone decides.
A program may use at most 64 MiB of HBM per device.

```python
import math
import jax
import jax.numpy as jnp
from jax import lax

LEVELS = 3
Z = 38
NX = 4096
NY = 4096


def shard_levels(rng, shape, pieces, smallest, largest):
    loudness, own = 1.0, jax.random.fold_in(rng, 6)
    for position, parts in pieces:
        heights = jnp.exp(jax.random.uniform(jax.random.fold_in(own, position), (parts,), jnp.float32, smallest / len(pieces), largest / len(pieces)))
        loudness = loudness * jnp.repeat(heights, shape[position] // parts).reshape([-1 if axis == position else 1 for axis in range(len(shape))])
    return loudness


def setup_inputs(seed: int = 0) -> dict:
    seeds = jax.random.split(jax.random.key(seed), 2)
    vorticity = jnp.clip(jnp.exp(math.log(20.0) - 5.9914645 * jax.random.uniform(seeds[0], (Z, NX, NY), jnp.float32) ** shard_levels(seeds[0], (Z, NX, NY), ((1, 32), (2, 32)), -0.2, 0.2)), 0.05, 20.0)
    return {"vorticity": vorticity}


LOW_TAPS = (0.3326705529509569, 0.8068915093133388, 0.4598775021193313, -0.13501102001039084, -0.08544127388224149, 0.035226291882100656)
HIGH_TAPS = (0.035226291882100656, 0.08544127388224149, -0.13501102001039084, -0.4598775021193313, 0.8068915093133388, -0.3326705529509569)


def split_axis(values, axis_dim):
    low_sum = jnp.zeros_like(values)
    high_sum = jnp.zeros_like(values)
    for tap_index in range(len(LOW_TAPS)):
        shifted = jnp.roll(values, -tap_index, axis=axis_dim)
        low_sum = low_sum + LOW_TAPS[tap_index] * shifted
        high_sum = high_sum + HIGH_TAPS[tap_index] * shifted
    length = values.shape[axis_dim]
    low_sum = lax.slice_in_dim(low_sum, 0, length, 2, axis_dim)
    high_sum = lax.slice_in_dim(high_sum, 0, length, 2, axis_dim)
    return low_sum, high_sum


def plane_details(plane):
    smooth = plane
    details = []
    for level_index in range(LEVELS):
        low_x, high_x = split_axis(smooth, 0)
        low_low, low_high = split_axis(low_x, 1)
        high_low, high_high = split_axis(high_x, 1)
        detail = jnp.maximum(jnp.maximum(jnp.abs(low_high), jnp.abs(high_low)), jnp.abs(high_high))
        details.append(detail)
        smooth = low_low
    return tuple(details)


def depth_max(values):
    return jnp.maximum(jnp.maximum(values[:-2], values[1:-1]), values[2:])


def pool_pairs(values):
    planes, size_x, size_y = values.shape
    return jnp.max(values.reshape(planes, size_x // 2, 2, size_y // 2, 2), axis=(2, 4))


def periodic_box(values):
    along_x = jnp.maximum(jnp.maximum(jnp.roll(values, 1, axis=1), values), jnp.roll(values, -1, axis=1))
    return jnp.maximum(jnp.maximum(jnp.roll(along_x, 1, axis=2), along_x), jnp.roll(along_x, -1, axis=2))


def reference(vorticity):
    details = lax.map(plane_details, vorticity)
    outputs = []
    carried = None
    for level_index in range(LEVELS):
        stacked = depth_max(details[level_index])
        if level_index > 0:
            stacked = jnp.maximum(stacked, pool_pairs(carried))
        carried = stacked
        outputs.append(periodic_box(stacked))
    return (outputs[0], outputs[1], outputs[2])
```

```python
import functools

import jax
import jax.numpy as jnp
from jax import lax
from jax.experimental import pallas as pl
from jax.experimental.pallas import tpu as pltpu
from jax.sharding import PartitionSpec as P

H = (
    0.3326705529509569,
    0.8068915093133388,
    0.4598775021193313,
    -0.13501102001039084,
    -0.08544127388224149,
    0.035226291882100656,
)
G = tuple((-1) ** t * H[5 - t] for t in range(6))
Z = 38
HALF = 20
BLK = 10
GRP = 3
HR = 4
CHUNKS = ((0, 10), (10, 20))
MESH = pl.DeviceIdType.MESH
roll = pltpu.roll


def lane_ids(rows):
    return lax.broadcasted_iota(jnp.int32, (rows, 128), 1)


def split(ref, lead, start, n):
    low = high = None
    for t in range(6):
        tap = ref[lead + (pl.ds(start + t, n, stride=2), slice(None))]
        low = tap * H[t] if low is None else low + tap * H[t]
        high = tap * G[t] if high is None else high + tap * G[t]
    return low, high


def pool_rows(ref, lead, start, n):
    return jnp.maximum(
        ref[lead + (pl.ds(start, n, stride=2), slice(None))],
        ref[lead + (pl.ds(start + 1, n, stride=2), slice(None))],
    )


def box_rows(ref, lead, n):
    return jnp.maximum(
        jnp.maximum(
            ref[lead + (pl.ds(7, n), slice(None))],
            ref[lead + (pl.ds(9, n), slice(None))],
        ),
        ref[lead + (pl.ds(8, n), slice(None))],
    )


def pair_of(q):
    return jnp.minimum(q + HALF, Z - 1)


def loop(lo, hi, body):
    def step(i, _):
        body(i)
        return 0

    lax.fori_loop(lo, hi, step, 0)


def kernel(
    v, o1, o2, o3,
    vb, tb, s1, d1, t2, s2, c2, pc, p1, t3, p2, c3, e1, y2, x3,
    f1y_s, f1y_r, f1x_s, f1x_r, f2x_s, f2x_r, f2y_s, f2y_r, f3y_s, f3y_r, f3x_s, f3x_r,
    in_sem, send_sem, recv_sem,
):
    nx, ny = lax.axis_size("gx"), lax.axis_size("gy")
    ix, iy = lax.axis_index("gx"), lax.axis_index("gy")
    x_prev = (lax.rem(ix + nx - 1, nx), iy)
    x_next = (lax.rem(ix + 1, nx), iy)
    y_prev = (ix, lax.rem(iy + ny - 1, ny))
    y_next = (ix, lax.rem(iy + 1, ny))
    counter = [0]

    def remote(src, dst, target):
        k = counter[0]
        counter[0] += 1
        return pltpu.make_async_remote_copy(
            src_ref=src, dst_ref=dst, send_sem=send_sem.at[k], recv_sem=recv_sem.at[k],
            device_id=target, device_id_type=MESH,
        )

    def frames(send, recv, prev, following):
        return [
            remote(send.at[0], recv.at[1], prev),
            remote(send.at[1], recv.at[0], following),
        ]

    spans = []
    for q0, q1 in CHUNKS:
        spans.append(((q0, q1), (q0 + HALF, min(q1 + HALF, Z))))
    loads, hx1, hy1 = [], [], []
    for number, pieces in enumerate(spans):
        row = []
        for part, (a, b) in enumerate(pieces):
            row.append(
                pltpu.make_async_copy(
                    v.at[pl.ds(a, b - a)], vb.at[pl.ds(a, b - a), pl.ds(0, 128)],
                    in_sem.at[2 * number + part],
                )
            )
        loads.append(row)
    for row in loads:
        for copy in row:
            copy.start()

    barrier = pltpu.get_barrier_semaphore()
    for device in (x_prev, x_next, y_prev, y_next):
        pl.semaphore_signal(barrier, inc=1, device_id=device, device_id_type=MESH)
    pl.semaphore_wait(barrier, 4)

    for pieces in spans:
        row = [
            remote(
                v.at[pl.ds(a, b - a), pl.ds(0, HR)],
                vb.at[pl.ds(a, b - a), pl.ds(128, HR)], x_prev,
            )
            for a, b in pieces
        ]
        for copy in row:
            copy.start()
        hx1.append(row)

    def stage_x1(p):
        lows, highs = [], []
        for piece in range(2):
            low, high = split(vb, (p,), 64 * piece, 32)
            lows.append(low)
            highs.append(high)
        tb[p, pl.ds(0, 128), :] = jnp.concatenate(lows + highs, axis=0).T

    for number, pieces in enumerate(spans):
        for copy in loads[number]:
            copy.wait()
        for copy in hx1[number]:
            copy.wait_recv()
        for a, b in pieces:
            loop(a, b, stage_x1)
        row = [
            remote(
                tb.at[pl.ds(a, b - a), pl.ds(0, HR)],
                tb.at[pl.ds(a, b - a), pl.ds(128, HR)], y_prev,
            )
            for a, b in pieces
        ]
        for copy in row:
            copy.start()
        hy1.append(row)

    first = lane_ids(32) < 64

    def stage_y1(q):
        other = pair_of(q)
        for piece in range(2):
            low_a, high_a = split(tb, (q,), 64 * piece, 32)
            low_b, high_b = split(tb, (other,), 64 * piece, 32)
            turned_a, turned_b = roll(low_a, 64, 1), roll(low_b, 64, 1)
            s1[q, pl.ds(32 * piece, 32), :] = jnp.where(first, low_a, turned_b)
            cross = jnp.abs(jnp.where(first, turned_a, low_b))
            high_a, high_b = jnp.abs(high_a), jnp.abs(high_b)
            high_a = jnp.maximum(high_a, roll(high_a, 64, 1))
            high_b = jnp.maximum(high_b, roll(high_b, 64, 1))
            detail = jnp.maximum(jnp.where(first, high_a, high_b), cross)
            d1[q, pl.ds(8 + 32 * piece, 32), :] = detail
            if piece == 0:
                f1y_s[0, q, :, :] = detail[0:1]
            else:
                f1y_s[1, q, :, :] = detail[31:32]

    hy2 = []
    for number, (q0, q1) in enumerate(CHUNKS):
        for copy in hy1[number]:
            copy.wait_recv()
        loop(q0, q1, stage_y1)
        copy = remote(
            s1.at[pl.ds(q0, q1 - q0), pl.ds(0, HR)],
            s1.at[pl.ds(q0, q1 - q0), pl.ds(64, HR)], y_prev,
        )
        copy.start()
        hy2.append(copy)
    f1y = frames(f1y_s, f1y_r, y_prev, y_next)
    for copy in f1y:
        copy.start()

    quarter = lax.rem(lane_ids(32), 64) < 32

    def stage_p1(b):
        rows = [pool_rows(d1, (b + 5 * k,), 8, 32) for k in range(4)]
        p1[b, :, :] = jnp.concatenate(rows, axis=0).T
        pool_a = pool_rows(p1, (b,), 0, 32)
        pool_b = pool_rows(p1, (b,), 64, 32)
        pc[b, :, :] = jnp.where(quarter, pool_a, roll(pool_b, 32, 1))
        pc[b + 5, :, :] = jnp.where(quarter, roll(pool_a, 96, 1), pool_b)

    loop(0, 5, stage_p1)

    def stage_y2(b):
        rows = []
        for q in (b, b + BLK):
            rows += split(s1, (q,), 0, 32)
        turned = jnp.concatenate(rows, axis=0).T
        t2[b, 0, pl.ds(0, 64), :] = turned[:64]
        t2[b, 1, pl.ds(0, 64), :] = turned[64:]

    for copy in hy2:
        copy.wait_recv()
    loop(0, BLK, stage_y2)
    hx2 = remote(
        t2.at[:, :, pl.ds(0, HR)], t2.at[:, :, pl.ds(64, HR)], x_prev
    )
    hx2.start()

    for copy in f1y:
        copy.wait_recv()

    def stage_l1y(b):
        rows = []
        for q in (b, b + BLK):
            d1[q, 7:8, :] = f1y_r[0, q, :, :]
            d1[q, 72:73, :] = f1y_r[1, q, :, :]
            rows.append(box_rows(d1, (q,), 64))
        turned = jnp.concatenate(rows, axis=0).T
        for k in range(2):
            e1[b, k, pl.ds(8, 64), :] = turned[64 * k : 64 * k + 64]
            f1x_s[0, b, k, :, :] = turned[64 * k : 64 * k + 1]
            f1x_s[1, b, k, :, :] = turned[64 * k + 63 : 64 * k + 64]

    loop(0, BLK, stage_l1y)
    f1x = frames(f1x_s, f1x_r, x_prev, x_next)
    for copy in f1x:
        copy.start()

    def stage_x2(b):
        lows, details = [], []
        for k in range(2):
            low, high = split(t2, (b, k), 0, 32)
            high = jnp.abs(high)
            lows.append(low)
            details.append(
                jnp.maximum(high, roll(jnp.maximum(jnp.abs(low), high), 96, 1))
            )
        s2[b, pl.ds(0, 32), :] = jnp.where(quarter, lows[0], roll(lows[1], 32, 1))
        detail = jnp.where(quarter, details[0], roll(details[1], 32, 1))
        detail = jnp.maximum(detail, pc[b, :, :])
        c2[b, pl.ds(8, 32), :] = detail
        f2x_s[0, b, :, :] = detail[0:1]
        f2x_s[1, b, :, :] = detail[31:32]

    hx2.wait_recv()
    loop(0, BLK, stage_x2)
    hx3 = remote(s2.at[:, pl.ds(0, HR)], s2.at[:, pl.ds(32, HR)], x_prev)
    hx3.start()
    f2x = frames(f2x_s, f2x_r, x_prev, x_next)
    for copy in f2x:
        copy.start()

    def blocks_of(c):
        return [jnp.minimum(4 * c + k, BLK - 1) for k in range(4)]

    def stage_p2(c):
        rows = []
        for b in blocks_of(c):
            pooled = pool_rows(c2, (b,), 8, 16)
            rows += [pooled, pooled]
        p2[c, :, :] = jnp.concatenate(rows, axis=0).T

    loop(0, GRP, stage_p2)

    for copy in f1x:
        copy.wait_recv()

    def stage_l1x(b):
        for k in range(2):
            e1[b, k, 7:8, :] = f1x_r[0, b, k, :, :]
            e1[b, k, 72:73, :] = f1x_r[1, b, k, :, :]
            boxed = box_rows(e1, (b, k), 64)
            o1[b + HALF * k, :, :] = boxed[:, :64]
            o1[b + HALF * k + BLK, :, :] = roll(boxed, 64, 1)[:, :64]

    def stage_x3(c):
        rows = []
        for b in blocks_of(c):
            rows += split(s2, (b,), 0, 16)
        turned = jnp.concatenate(rows, axis=0).T
        for g in range(4):
            t3[c, g, pl.ds(0, 32), :] = turned[32 * g : 32 * g + 32]

    hx3.wait_recv()
    loop(0, GRP, stage_x3)
    hy3 = remote(
        t3.at[:, :, pl.ds(0, HR)], t3.at[:, :, pl.ds(32, HR)], y_prev
    )
    hy3.start()

    loop(0, BLK // 2, stage_l1x)

    for copy in f2x:
        copy.wait_recv()

    def stage_l2x(c):
        rows = []
        for b in blocks_of(c):
            c2[b, 7:8, :] = f2x_r[0, b, :, :]
            c2[b, 40:41, :] = f2x_r[1, b, :, :]
            rows.append(box_rows(c2, (b,), 32))
        turned = jnp.concatenate(rows, axis=0).T
        for g in range(4):
            y2[c, g, pl.ds(8, 32), :] = turned[32 * g : 32 * g + 32]
            f2y_s[0, c, g, :, :] = turned[32 * g : 32 * g + 1]
            f2y_s[1, c, g, :, :] = turned[32 * g + 31 : 32 * g + 32]

    loop(0, GRP, stage_l2x)
    f2y = frames(f2y_s, f2y_r, y_prev, y_next)
    for copy in f2y:
        copy.start()

    def stage_y3(c):
        for g in range(4):
            low, high = split(t3, (c, g), 0, 16)
            high = jnp.abs(high)
            detail = jnp.maximum(high, roll(jnp.maximum(jnp.abs(low), high), 112, 1))
            detail = jnp.maximum(detail, pool_rows(p2, (c,), 32 * g, 16))
            c3[c, g, pl.ds(8, 16), :] = detail
            f3y_s[0, c, g, :, :] = detail[0:1]
            f3y_s[1, c, g, :, :] = detail[15:16]

    hy3.wait_recv()
    loop(0, GRP, stage_y3)
    f3y = frames(f3y_s, f3y_r, y_prev, y_next)
    for copy in f3y:
        copy.start()

    loop(BLK // 2, BLK, stage_l1x)

    for copy in f3y:
        copy.wait_recv()

    def stage_l3y(c):
        rows = []
        for g in range(4):
            c3[c, g, 7:8, :] = f3y_r[0, c, g, :, :]
            c3[c, g, 24:25, :] = f3y_r[1, c, g, :, :]
            rows.append(box_rows(c3, (c, g), 16))
        turned = jnp.concatenate(rows + rows, axis=0).T
        for k in range(4):
            x3[c, k, pl.ds(8, 16), :] = turned[32 * k : 32 * k + 16]
            f3x_s[0, c, k, :, :] = turned[32 * k : 32 * k + 1]
            f3x_s[1, c, k, :, :] = turned[32 * k + 15 : 32 * k + 16]

    loop(0, GRP, stage_l3y)
    f3x = frames(f3x_s, f3x_r, x_prev, x_next)
    for copy in f3x:
        copy.start()

    for copy in f2y:
        copy.wait_recv()

    offsets = (0, HALF, BLK, HALF + BLK)
    for c in range(GRP):
        rows = []
        for g in range(4):
            y2[c, g, 7:8, :] = f2y_r[0, c, g, :, :]
            y2[c, g, 40:41, :] = f2y_r[1, c, g, :, :]
            rows.append(box_rows(y2, (c, g), 32))
        turned = jnp.concatenate(rows, axis=0).T
        for k in range(min(4, BLK - 4 * c)):
            block = turned[32 * k : 32 * k + 32]
            for g in range(4):
                spun = roll(block, 128 - 32 * g, 1) if g else block
                o2[4 * c + k + offsets[g], :, :] = spun[:, :32]

    for copy in f3x:
        copy.wait_recv()
    for c in range(GRP):
        for k in range(min(4, BLK - 4 * c)):
            x3[c, k, 7:8, :] = f3x_r[0, c, k, :, :]
            x3[c, k, 24:25, :] = f3x_r[1, c, k, :, :]
            block = box_rows(x3, (c, k), 16)
            for g in range(4):
                spun = roll(block, 128 - 16 * g, 1) if g else block
                o3[4 * c + k + offsets[g], :, :] = spun[:, :16]

    for row in hx1 + hy1 + [hy2, f1y, [hx2], f1x, [hx3], f2x, [hy3], f2y, f3y, f3x]:
        for copy in row:
            copy.wait_send()


def deepest(values):
    count = Z - 2
    return jnp.maximum(
        jnp.maximum(values[:count], values[1 : count + 1]), values[2 : count + 2]
    )


def shards(vorticity):
    f32 = jnp.float32
    copies = 4 * len(CHUNKS) + len(CHUNKS) + 4 + 12
    rows = lambda *shape: pltpu.VMEM(shape, f32)
    frame = lambda *shape: [pltpu.VMEM((2,) + shape + (1, 128), f32)] * 2
    planes = 2 * HALF
    o1, o2, o3 = pl.pallas_call(
        kernel,
        out_shape=[
            jax.ShapeDtypeStruct((planes, 64, 64), f32),
            jax.ShapeDtypeStruct((planes, 32, 32), f32),
            jax.ShapeDtypeStruct((planes, 16, 16), f32),
        ],
        in_specs=[pl.BlockSpec(memory_space=pl.ANY)],
        out_specs=[pl.BlockSpec(memory_space=pltpu.VMEM)] * 3,
        scratch_shapes=[
            rows(Z, 136, 128),
            rows(Z, 136, 128),
            rows(HALF, 72, 128),
            rows(HALF, 80, 128),
            rows(BLK, 2, 72, 128),
            rows(BLK, 40, 128),
            rows(BLK, 48, 128),
            rows(BLK, 32, 128),
            rows(5, 128, 128),
            rows(GRP, 4, 40, 128),
            rows(GRP, 128, 128),
            rows(GRP, 4, 32, 128),
            rows(BLK, 2, 80, 128),
            rows(GRP, 4, 48, 128),
            rows(GRP, 4, 32, 128),
            *frame(HALF),
            *frame(BLK, 2),
            *frame(BLK),
            *frame(GRP, 4),
            *frame(GRP, 4),
            *frame(GRP, 4),
            pltpu.SemaphoreType.DMA((2 * len(CHUNKS),)),
            pltpu.SemaphoreType.DMA((copies,)),
            pltpu.SemaphoreType.DMA((copies,)),
        ],
        compiler_params=pltpu.CompilerParams(
            collective_id=0, has_side_effects=True, vmem_limit_bytes=40 * 2**20
        ),
    )(vorticity)
    return deepest(o1), deepest(o2), deepest(o3)


def solution(mesh):
    placed = P(None, "gx", "gy")
    return jax.shard_map(
        shards, mesh=mesh, in_specs=(placed,), out_specs=(placed,) * 3, check_vma=False
    )
```

```python
import functools

import jax
import jax.numpy as jnp
from jax import lax
from jax.experimental import pallas as pl
from jax.experimental.pallas import tpu as pltpu
from jax.sharding import PartitionSpec as P

H = (
    0.3326705529509569,
    0.8068915093133388,
    0.4598775021193313,
    -0.13501102001039084,
    -0.08544127388224149,
    0.035226291882100656,
)
G = tuple((-1) ** t * H[5 - t] for t in range(6))
Z = 38
HALF = 20
BLK = 10
GRP = 3
HR = 4
OUT = Z - 2
PITCH = 48
UNROLL = 5
CHUNKS = ((0, 10), (10, 20))
MESH = pl.DeviceIdType.MESH
roll = pltpu.roll


def lane_ids(rows):
    return lax.broadcasted_iota(jnp.int32, (rows, 128), 1)


def split(ref, lead, start, n):
    low = high = None
    for t in range(6):
        tap = ref[lead + (pl.ds(start + t, n, stride=2), slice(None))]
        low = tap * H[t] if low is None else low + tap * H[t]
        high = tap * G[t] if high is None else high + tap * G[t]
    return low, high


def pool_rows(ref, lead, start, n):
    return jnp.maximum(
        ref[lead + (pl.ds(start, n, stride=2), slice(None))],
        ref[lead + (pl.ds(start + 1, n, stride=2), slice(None))],
    )


def box_rows(ref, lead, n):
    return jnp.maximum(
        jnp.maximum(
            ref[lead + (pl.ds(7, n), slice(None))],
            ref[lead + (pl.ds(9, n), slice(None))],
        ),
        ref[lead + (pl.ds(8, n), slice(None))],
    )


def pair_of(q):
    return jnp.minimum(q + HALF, Z - 1)


def loop(lo, hi, body):
    def step(i, _):
        body(i)
        return 0

    lax.fori_loop(lo, hi, step, 0, unroll=min(UNROLL, hi - lo))


def kernel(
    v, o1, o2, o3,
    vb, tb, s1, d1, t2, s2, c2, pc, p1, t3, p2, c3, e1, eb, y2, w2, x3, w3,
    f1y_s, f1y_r, f1x_s, f1x_r, f2x_s, f2x_r, f2y_s, f2y_r, f3y_s, f3y_r, f3x_s, f3x_r,
    in_sem, send_sem, recv_sem,
):
    nx, ny = lax.axis_size("gx"), lax.axis_size("gy")
    ix, iy = lax.axis_index("gx"), lax.axis_index("gy")
    x_prev = (lax.rem(ix + nx - 1, nx), iy)
    x_next = (lax.rem(ix + 1, nx), iy)
    y_prev = (ix, lax.rem(iy + ny - 1, ny))
    y_next = (ix, lax.rem(iy + 1, ny))
    counter = [0]

    def remote(src, dst, target):
        k = counter[0]
        counter[0] += 1
        return pltpu.make_async_remote_copy(
            src_ref=src, dst_ref=dst, send_sem=send_sem.at[k], recv_sem=recv_sem.at[k],
            device_id=target, device_id_type=MESH,
        )

    def frames(send, recv, prev, following):
        return [
            remote(send.at[0], recv.at[1], prev),
            remote(send.at[1], recv.at[0], following),
        ]

    spans = []
    for q0, q1 in CHUNKS:
        spans.append(((q0, q1), (q0 + HALF, min(q1 + HALF, Z))))
    loads, hx1, hy1 = [], [], []
    for number, pieces in enumerate(spans):
        row = []
        for part, (a, b) in enumerate(pieces):
            row.append(
                pltpu.make_async_copy(
                    v.at[pl.ds(a, b - a)], vb.at[pl.ds(a, b - a), pl.ds(0, 128)],
                    in_sem.at[2 * number + part],
                )
            )
        loads.append(row)
    for row in loads:
        for copy in row:
            copy.start()

    barrier = pltpu.get_barrier_semaphore()
    for device in (x_prev, x_next, y_prev, y_next):
        pl.semaphore_signal(barrier, inc=1, device_id=device, device_id_type=MESH)
    pl.semaphore_wait(barrier, 4)

    for pieces in spans:
        row = [
            remote(
                v.at[pl.ds(a, b - a), pl.ds(0, HR)],
                vb.at[pl.ds(a, b - a), pl.ds(128, HR)], x_prev,
            )
            for a, b in pieces
        ]
        for copy in row:
            copy.start()
        hx1.append(row)

    def stage_x1(p):
        lows, highs = [], []
        for piece in range(2):
            low, high = split(vb, (p,), 64 * piece, 32)
            lows.append(low)
            highs.append(high)
        tb[p, pl.ds(0, 128), :] = jnp.concatenate(lows + highs, axis=0).T

    for number, pieces in enumerate(spans):
        for copy in loads[number]:
            copy.wait()
        for copy in hx1[number]:
            copy.wait_recv()
        for a, b in pieces:
            loop(a, b, stage_x1)
        row = [
            remote(
                tb.at[pl.ds(a, b - a), pl.ds(0, HR)],
                tb.at[pl.ds(a, b - a), pl.ds(128, HR)], y_prev,
            )
            for a, b in pieces
        ]
        for copy in row:
            copy.start()
        hy1.append(row)

    first = lane_ids(32) < 64

    def stage_y1(q):
        other = pair_of(q)
        for piece in range(2):
            low_a, high_a = split(tb, (q,), 64 * piece, 32)
            low_b, high_b = split(tb, (other,), 64 * piece, 32)
            turned_a, turned_b = roll(low_a, 64, 1), roll(low_b, 64, 1)
            s1[q, pl.ds(32 * piece, 32), :] = jnp.where(first, low_a, turned_b)
            cross = jnp.abs(jnp.where(first, turned_a, low_b))
            high_a, high_b = jnp.abs(high_a), jnp.abs(high_b)
            high_a = jnp.maximum(high_a, roll(high_a, 64, 1))
            high_b = jnp.maximum(high_b, roll(high_b, 64, 1))
            detail = jnp.maximum(jnp.where(first, high_a, high_b), cross)
            d1[q, pl.ds(8 + 32 * piece, 32), :] = detail
            if piece == 0:
                f1y_s[0, q, :, :] = detail[0:1]
            else:
                f1y_s[1, q, :, :] = detail[31:32]

    hy2 = []
    for number, (q0, q1) in enumerate(CHUNKS):
        for copy in hy1[number]:
            copy.wait_recv()
        loop(q0, q1, stage_y1)
        copy = remote(
            s1.at[pl.ds(q0, q1 - q0), pl.ds(0, HR)],
            s1.at[pl.ds(q0, q1 - q0), pl.ds(64, HR)], y_prev,
        )
        copy.start()
        hy2.append(copy)
    f1y = frames(f1y_s, f1y_r, y_prev, y_next)
    for copy in f1y:
        copy.start()

    quarter = lax.rem(lane_ids(32), 64) < 32

    def stage_p1(b):
        rows = [pool_rows(d1, (b + 5 * k,), 8, 32) for k in range(4)]
        p1[b, :, :] = jnp.concatenate(rows, axis=0).T
        pool_a = pool_rows(p1, (b,), 0, 32)
        pool_b = pool_rows(p1, (b,), 64, 32)
        pc[b, :, :] = jnp.where(quarter, pool_a, roll(pool_b, 32, 1))
        pc[b + 5, :, :] = jnp.where(quarter, roll(pool_a, 96, 1), pool_b)

    loop(0, 5, stage_p1)

    def stage_y2(b):
        rows = []
        for q in (b, b + BLK):
            rows += split(s1, (q,), 0, 32)
        turned = jnp.concatenate(rows, axis=0).T
        t2[b, 0, pl.ds(0, 64), :] = turned[:64]
        t2[b, 1, pl.ds(0, 64), :] = turned[64:]

    for copy in hy2:
        copy.wait_recv()
    loop(0, BLK, stage_y2)
    hx2 = remote(
        t2.at[:, :, pl.ds(0, HR)], t2.at[:, :, pl.ds(64, HR)], x_prev
    )
    hx2.start()

    for copy in f1y:
        copy.wait_recv()

    def stage_l1y(b):
        rows = []
        for q in (b, b + BLK):
            d1[q, 7:8, :] = f1y_r[0, q, :, :]
            d1[q, 72:73, :] = f1y_r[1, q, :, :]
            rows.append(box_rows(d1, (q,), 64))
        turned = jnp.concatenate(rows, axis=0).T
        for k in range(2):
            e1[b, k, pl.ds(8, 64), :] = turned[64 * k : 64 * k + 64]
            f1x_s[0, b, k, :, :] = turned[64 * k : 64 * k + 1]
            f1x_s[1, b, k, :, :] = turned[64 * k + 63 : 64 * k + 64]

    loop(0, BLK, stage_l1y)
    f1x = frames(f1x_s, f1x_r, x_prev, x_next)
    for copy in f1x:
        copy.start()

    def stage_x2(b):
        lows, details = [], []
        for k in range(2):
            low, high = split(t2, (b, k), 0, 32)
            high = jnp.abs(high)
            lows.append(low)
            details.append(
                jnp.maximum(high, roll(jnp.maximum(jnp.abs(low), high), 96, 1))
            )
        s2[b, pl.ds(0, 32), :] = jnp.where(quarter, lows[0], roll(lows[1], 32, 1))
        detail = jnp.where(quarter, details[0], roll(details[1], 32, 1))
        detail = jnp.maximum(detail, pc[b, :, :])
        c2[b, pl.ds(8, 32), :] = detail
        f2x_s[0, b, :, :] = detail[0:1]
        f2x_s[1, b, :, :] = detail[31:32]

    hx2.wait_recv()
    loop(0, BLK, stage_x2)
    hx3 = remote(s2.at[:, pl.ds(0, HR)], s2.at[:, pl.ds(32, HR)], x_prev)
    hx3.start()
    f2x = frames(f2x_s, f2x_r, x_prev, x_next)
    for copy in f2x:
        copy.start()

    def blocks_of(c):
        return [jnp.minimum(4 * c + k, BLK - 1) for k in range(4)]

    def stage_p2(c):
        rows = []
        for b in blocks_of(c):
            pooled = pool_rows(c2, (b,), 8, 16)
            rows += [pooled, pooled]
        p2[c, :, :] = jnp.concatenate(rows, axis=0).T

    loop(0, GRP, stage_p2)

    for copy in f1x:
        copy.wait_recv()

    def stage_l1x(b):
        for k in range(2):
            e1[b, k, 7:8, :] = f1x_r[0, b, k, :, :]
            e1[b, k, 72:73, :] = f1x_r[1, b, k, :, :]
            eb[b, k, :, :] = box_rows(e1, (b, k), 64)

    def deep(b, k):
        return jnp.maximum(jnp.maximum(eb[b, k], eb[b + 1, k]), eb[b + 2, k])

    def stage_o1(b):
        for k in range(2):
            deepest = deep(b, k)
            o1[b + HALF * k, :, :] = deepest[:, :64]
            if k == 0:
                o1[b + BLK, :, :] = roll(deepest, 64, 1)[:, :64]

    def stage_o1_rest(b):
        o1[b + HALF + BLK, :, :] = roll(deep(b, 1), 64, 1)[:, :64]

    def finish_l1():
        half = lane_ids(64) < 64
        for b in range(2):
            later = roll(eb[b, 1], 64, 1)
            eb[BLK + b, 0] = jnp.where(half, roll(eb[b, 0], 64, 1), later)
            eb[BLK + b, 1] = later
        loop(0, BLK, stage_o1)
        loop(0, OUT - HALF - BLK, stage_o1_rest)

    def stage_x3(c):
        rows = []
        for b in blocks_of(c):
            rows += split(s2, (b,), 0, 16)
        turned = jnp.concatenate(rows, axis=0).T
        for g in range(4):
            t3[c, g, pl.ds(0, 32), :] = turned[32 * g : 32 * g + 32]

    hx3.wait_recv()
    loop(0, GRP, stage_x3)
    hy3 = remote(
        t3.at[:, :, pl.ds(0, HR)], t3.at[:, :, pl.ds(32, HR)], y_prev
    )
    hy3.start()

    loop(0, BLK // 2, stage_l1x)

    for copy in f2x:
        copy.wait_recv()

    def stage_l2x(c):
        rows = []
        for b in blocks_of(c):
            c2[b, 7:8, :] = f2x_r[0, b, :, :]
            c2[b, 40:41, :] = f2x_r[1, b, :, :]
            rows.append(box_rows(c2, (b,), 32))
        turned = jnp.concatenate(rows, axis=0).T
        for g in range(4):
            y2[c, g, pl.ds(8, 32), :] = turned[32 * g : 32 * g + 32]
            f2y_s[0, c, g, :, :] = turned[32 * g : 32 * g + 1]
            f2y_s[1, c, g, :, :] = turned[32 * g + 31 : 32 * g + 32]

    loop(0, GRP, stage_l2x)
    f2y = frames(f2y_s, f2y_r, y_prev, y_next)
    for copy in f2y:
        copy.start()

    def stage_y3(c):
        for g in range(4):
            low, high = split(t3, (c, g), 0, 16)
            high = jnp.abs(high)
            detail = jnp.maximum(high, roll(jnp.maximum(jnp.abs(low), high), 112, 1))
            detail = jnp.maximum(detail, pool_rows(p2, (c,), 32 * g, 16))
            c3[c, g, pl.ds(8, 16), :] = detail
            f3y_s[0, c, g, :, :] = detail[0:1]
            f3y_s[1, c, g, :, :] = detail[15:16]

    hy3.wait_recv()
    loop(0, GRP, stage_y3)
    f3y = frames(f3y_s, f3y_r, y_prev, y_next)
    for copy in f3y:
        copy.start()

    loop(BLK // 2, BLK, stage_l1x)
    finish_l1()

    for copy in f3y:
        copy.wait_recv()

    def stage_l3y(c):
        rows = []
        for g in range(4):
            c3[c, g, 7:8, :] = f3y_r[0, c, g, :, :]
            c3[c, g, 24:25, :] = f3y_r[1, c, g, :, :]
            rows.append(box_rows(c3, (c, g), 16))
        turned = jnp.concatenate(rows + rows, axis=0).T
        for k in range(4):
            x3[c, k, pl.ds(8, 16), :] = turned[32 * k : 32 * k + 16]
            f3x_s[0, c, k, :, :] = turned[32 * k : 32 * k + 1]
            f3x_s[1, c, k, :, :] = turned[32 * k + 15 : 32 * k + 16]

    loop(0, GRP, stage_l3y)
    f3x = frames(f3x_s, f3x_r, x_prev, x_next)
    for copy in f3x:
        copy.start()

    for copy in f2y:
        copy.wait_recv()

    offsets = (0, HALF, BLK, HALF + BLK)
    for c in range(GRP):
        rows = []
        for g in range(4):
            y2[c, g, 7:8, :] = f2y_r[0, c, g, :, :]
            y2[c, g, 40:41, :] = f2y_r[1, c, g, :, :]
            rows.append(box_rows(y2, (c, g), 32))
        turned = jnp.concatenate(rows, axis=0).T
        for k in range(min(4, BLK - 4 * c)):
            block = turned[32 * k : 32 * k + 32]
            for g in range(4):
                spun = roll(block, 128 - 32 * g, 1) if g else block
                w2[pl.ds(4 * c + k + offsets[g], 32, stride=PITCH), :] = spun

    def planes_last(w, x, n):
        start = pl.multiple_of(x * PITCH, 8)
        deepest = w[pl.ds(start, 40), :]
        for shift in (1, 2):
            deepest = jnp.maximum(deepest, w[pl.ds(start + shift, 40), :])
        return deepest.T[:n, :OUT]

    def stage_o2(x):
        o2[x, :, :] = planes_last(w2, x, 32)

    loop(0, 32, stage_o2)

    for copy in f3x:
        copy.wait_recv()
    for c in range(GRP):
        for k in range(min(4, BLK - 4 * c)):
            x3[c, k, 7:8, :] = f3x_r[0, c, k, :, :]
            x3[c, k, 24:25, :] = f3x_r[1, c, k, :, :]
            block = box_rows(x3, (c, k), 16)
            for g in range(4):
                spun = roll(block, 128 - 16 * g, 1) if g else block
                w3[pl.ds(4 * c + k + offsets[g], 16, stride=PITCH), :] = spun

    def stage_o3(x):
        o3[x, :, :] = planes_last(w3, x, 16)

    loop(0, 16, stage_o3)

    for row in hx1 + hy1 + [hy2, f1y, [hx2], f1x, [hx3], f2x, [hy3], f2y, f3y, f3x]:
        for copy in row:
            copy.wait_send()


def shards(vorticity):
    f32 = jnp.float32
    copies = 4 * len(CHUNKS) + len(CHUNKS) + 4 + 12
    rows = lambda *shape: pltpu.VMEM(shape, f32)
    frame = lambda *shape: [pltpu.VMEM((2,) + shape + (1, 128), f32)] * 2
    o1, o2, o3 = pl.pallas_call(
        kernel,
        out_shape=[
            jax.ShapeDtypeStruct((OUT, 64, 64), f32),
            jax.ShapeDtypeStruct((32, 32, OUT), f32),
            jax.ShapeDtypeStruct((16, 16, OUT), f32),
        ],
        in_specs=[pl.BlockSpec(memory_space=pltpu.HBM)],
        out_specs=[pl.BlockSpec(memory_space=pltpu.VMEM)] * 3,
        scratch_shapes=[
            rows(Z, 136, 128),
            rows(Z, 136, 128),
            rows(HALF, 72, 128),
            rows(HALF, 80, 128),
            rows(BLK, 2, 72, 128),
            rows(BLK, 40, 128),
            rows(BLK, 48, 128),
            rows(BLK, 32, 128),
            rows(5, 128, 128),
            rows(GRP, 4, 40, 128),
            rows(GRP, 128, 128),
            rows(GRP, 4, 32, 128),
            rows(BLK, 2, 80, 128),
            rows(BLK + 2, 2, 64, 128),
            rows(GRP, 4, 48, 128),
            rows(32 * PITCH, 128),
            rows(GRP, 4, 32, 128),
            rows(16 * PITCH, 128),
            *frame(HALF),
            *frame(BLK, 2),
            *frame(BLK),
            *frame(GRP, 4),
            *frame(GRP, 4),
            *frame(GRP, 4),
            pltpu.SemaphoreType.DMA((2 * len(CHUNKS),)),
            pltpu.SemaphoreType.DMA((copies,)),
            pltpu.SemaphoreType.DMA((copies,)),
        ],
        compiler_params=pltpu.CompilerParams(
            collective_id=0, has_side_effects=True, vmem_limit_bytes=51 * 2**20
        ),
    )(vorticity)
    return o1, jnp.transpose(o2, (2, 0, 1)), jnp.transpose(o3, (2, 0, 1))


def solution(mesh):
    placed = P(None, "gx", "gy")
    return jax.shard_map(
        shards, mesh=mesh, in_specs=(placed,), out_specs=(placed,) * 3, check_vma=False
    )
```

```python
import functools

import jax
import jax.numpy as jnp
from jax import lax
from jax.experimental import pallas as pl
from jax.experimental.pallas import tpu as pltpu
from jax.sharding import PartitionSpec as P

H = (
    0.3326705529509569,
    0.8068915093133388,
    0.4598775021193313,
    -0.13501102001039084,
    -0.08544127388224149,
    0.035226291882100656,
)
G = tuple((-1) ** t * H[5 - t] for t in range(6))
Z = 38
HALF = 20
BLK = 10
QUAD = 3
TWO = 5
HR = 4
OUT = Z - 2
PITCH = 48
UNROLL = 5
CHUNKS = ((0, 10), (10, 20))
MESH = pl.DeviceIdType.MESH
roll = pltpu.roll


def lane_ids(rows):
    return lax.broadcasted_iota(jnp.int32, (rows, 128), 1)


def split(ref, lead, start, n):
    low = high = None
    for t in range(6):
        tap = ref[lead + (pl.ds(start + t, n, stride=2), slice(None))]
        low = tap * H[t] if low is None else low + tap * H[t]
        high = tap * G[t] if high is None else high + tap * G[t]
    return low, high


def pool_rows(ref, lead, start, n):
    return jnp.maximum(
        ref[lead + (pl.ds(start, n, stride=2), slice(None))],
        ref[lead + (pl.ds(start + 1, n, stride=2), slice(None))],
    )


def box_rows(ref, lead, n):
    return jnp.maximum(
        jnp.maximum(
            ref[lead + (pl.ds(7, n), slice(None))],
            ref[lead + (pl.ds(9, n), slice(None))],
        ),
        ref[lead + (pl.ds(8, n), slice(None))],
    )


def pair_of(q):
    return jnp.minimum(q + HALF, Z - 1)


def loop(lo, hi, body):
    def step(i, _):
        body(i)
        return 0

    lax.fori_loop(lo, hi, step, 0, unroll=min(UNROLL, hi - lo))


def kernel(
    v, o1, o2, o3,
    vb, tb, s1, d1, t2, s2, c2, pc, p1, t3, p2, p3, c3, e1, eb, y2, w2, x3, w3,
    lk_s, lk_r, lh, f1y_s, f1y_r, f1x_s, f1x_r, fp_s, fp_r, f2y_s, f2y_r, f3p_s, f3p_r, t3_s, t3_r,
    in_sem, send_sem, recv_sem,
):
    nx, ny = lax.axis_size("gx"), lax.axis_size("gy")
    ix, iy = lax.axis_index("gx"), lax.axis_index("gy")
    x_prev = (lax.rem(ix + nx - 1, nx), iy)
    x_next = (lax.rem(ix + 1, nx), iy)
    y_prev = (ix, lax.rem(iy + ny - 1, ny))
    y_next = (ix, lax.rem(iy + 1, ny))
    counter = [0]

    def remote(src, dst, target):
        k = counter[0]
        counter[0] += 1
        return pltpu.make_async_remote_copy(
            src_ref=src, dst_ref=dst, send_sem=send_sem.at[k], recv_sem=recv_sem.at[k],
            device_id=target, device_id_type=MESH,
        )

    def frames(send, recv, prev, following):
        return [
            remote(send.at[0], recv.at[1], prev),
            remote(send.at[1], recv.at[0], following),
        ]

    spans = []
    for q0, q1 in CHUNKS:
        spans.append(((q0, q1), (q0 + HALF, min(q1 + HALF, Z))))
    loads, hx1, hy1 = [], [], []
    for number, pieces in enumerate(spans):
        row = []
        for part, (a, b) in enumerate(pieces):
            row.append(
                pltpu.make_async_copy(
                    v.at[pl.ds(a, b - a)], vb.at[pl.ds(a, b - a), pl.ds(0, 128)],
                    in_sem.at[2 * number + part],
                )
            )
        loads.append(row)
    for row in loads:
        for copy in row:
            copy.start()

    barrier = pltpu.get_barrier_semaphore()
    for device in (x_prev, x_next, y_prev, y_next):
        pl.semaphore_signal(barrier, inc=1, device_id=device, device_id_type=MESH)
    pl.semaphore_wait(barrier, 4)

    for pieces in spans:
        row = [
            remote(
                v.at[pl.ds(a, b - a), pl.ds(0, HR)],
                vb.at[pl.ds(a, b - a), pl.ds(128, HR)], x_prev,
            )
            for a, b in pieces
        ]
        for copy in row:
            copy.start()
        hx1.append(row)

    def stage_x1(p):
        lows, highs = [], []
        for piece in range(2):
            low, high = split(vb, (p,), 64 * piece, 32)
            lows.append(low)
            highs.append(high)
        tb[p, pl.ds(0, 128), :] = jnp.concatenate(lows + highs, axis=0).T

    def both(ref, q, start, n):
        later = roll(ref[pair_of(q), pl.ds(start, n), :], 64, 1)
        return jnp.where(lane_ids(n) < 64, ref[q, pl.ds(start, n), :], later)

    def stage_k1(q):
        lk_s[q, :, :] = both(tb, q, HR, 8)

    for number, pieces in enumerate(spans):
        for copy in loads[number]:
            copy.wait()
        for copy in hx1[number]:
            copy.wait_recv()
        for a, b in pieces:
            loop(a, b, stage_x1)
        row = [
            remote(
                tb.at[pl.ds(a, b - a), pl.ds(0, HR)],
                tb.at[pl.ds(a, b - a), pl.ds(128, HR)], y_prev,
            )
            for a, b in pieces
        ]
        for copy in row:
            copy.start()
        q0, q1 = CHUNKS[number]
        loop(q0, q1, stage_k1)
        copy = remote(lk_s.at[pl.ds(q0, q1 - q0)], lk_r.at[pl.ds(q0, q1 - q0)], y_prev)
        copy.start()
        hy1.append(row + [copy])

    first = lane_ids(32) < 64

    def stage_y1(q):
        other = pair_of(q)
        for piece in range(2):
            low_a, high_a = split(tb, (q,), 64 * piece, 32)
            low_b, high_b = split(tb, (other,), 64 * piece, 32)
            turned_a, turned_b = roll(low_a, 64, 1), roll(low_b, 64, 1)
            s1[q, pl.ds(32 * piece, 32), :] = jnp.where(first, low_a, turned_b)
            cross = jnp.abs(jnp.where(first, turned_a, low_b))
            high_a, high_b = jnp.abs(high_a), jnp.abs(high_b)
            high_a = jnp.maximum(high_a, roll(high_a, 64, 1))
            high_b = jnp.maximum(high_b, roll(high_b, 64, 1))
            detail = jnp.maximum(jnp.where(first, high_a, high_b), cross)
            d1[q, pl.ds(8 + 32 * piece, 32), :] = detail
            if piece == 0:
                f1y_s[0, q, :, :] = detail[0:1]
            else:
                f1y_s[1, q, :, :] = detail[31:32]

    def stage_k2(q):
        lh[q, pl.ds(0, HR), :] = both(tb, q, 128, HR)
        lh[q, pl.ds(HR, 8), :] = lk_r[q, :, :]
        low = None
        for t in range(6):
            tap = lh[q, pl.ds(t, HR, stride=2), :] * H[t]
            low = tap if low is None else low + tap
        s1[q, pl.ds(64, HR), :] = low

    for number, (q0, q1) in enumerate(CHUNKS):
        for copy in hy1[number]:
            copy.wait_recv()
        loop(q0, q1, stage_y1)
        loop(q0, q1, stage_k2)
    f1y = frames(f1y_s, f1y_r, y_prev, y_next)
    for copy in f1y:
        copy.start()

    quarter = lax.rem(lane_ids(32), 64) < 32

    def stage_p1(b):
        rows = [pool_rows(d1, (b + 5 * k,), 8, 32) for k in range(4)]
        p1[b, :, :] = jnp.concatenate(rows, axis=0).T
        pool_a = pool_rows(p1, (b,), 0, 32)
        pool_b = pool_rows(p1, (b,), 64, 32)
        for block, pooled in (
            (b, jnp.where(quarter, pool_a, roll(pool_b, 32, 1))),
            (b + 5, jnp.where(quarter, roll(pool_a, 96, 1), pool_b)),
        ):
            pc[block, pl.ds(8, 32), :] = pooled
            fp_s[0, block, :, :] = pooled[0:2]
            fp_s[1, block, :, :] = pooled[30:32]

    def stage_y2(b):
        rows = []
        for q in (b, b + BLK):
            rows += split(s1, (q,), 0, 32)
        turned = jnp.concatenate(rows, axis=0).T
        t2[b, 0, pl.ds(8, 64), :] = turned[:64]
        t2[b, 1, pl.ds(8, 64), :] = turned[64:]

    loop(0, BLK, stage_y2)
    hx2 = [
        remote(t2.at[:, :, pl.ds(8, 16)], t2.at[:, :, pl.ds(72, 16)], x_prev),
        remote(t2.at[:, :, pl.ds(64, 8)], t2.at[:, :, pl.ds(0, 8)], x_next),
    ]
    for copy in hx2:
        copy.start()
    loop(0, 5, stage_p1)
    fp = frames(fp_s, fp_r, x_prev, x_next)
    for copy in fp:
        copy.start()

    for copy in f1y:
        copy.wait_recv()

    def stage_l1y(b):
        rows = []
        for q in (b, b + BLK):
            d1[q, 7:8, :] = f1y_r[0, q, :, :]
            d1[q, 72:73, :] = f1y_r[1, q, :, :]
            rows.append(box_rows(d1, (q,), 64))
        turned = jnp.concatenate(rows, axis=0).T
        for k in range(2):
            e1[b, k, pl.ds(8, 64), :] = turned[64 * k : 64 * k + 64]
            f1x_s[0, b, k, :, :] = turned[64 * k : 64 * k + 1]
            f1x_s[1, b, k, :, :] = turned[64 * k + 63 : 64 * k + 64]

    loop(0, BLK, stage_l1y)
    f1x = frames(f1x_s, f1x_r, x_prev, x_next)
    for copy in f1x:
        copy.start()

    wide = lax.rem(lane_ids(40), 64) < 32

    def stage_x2(b):
        pc[b, 6:8, :] = fp_r[0, b, :, :]
        pc[b, 40:42, :] = fp_r[1, b, :, :]
        lows, details = [], []
        for k in range(2):
            low, high = split(t2, (b, k), 4, 40)
            high = jnp.abs(high)
            lows.append(low)
            details.append(
                jnp.maximum(high, roll(jnp.maximum(jnp.abs(low), high), 96, 1))
            )
        s2[b, pl.ds(0, 40), :] = jnp.where(wide, lows[0], roll(lows[1], 32, 1))
        detail = jnp.where(wide, details[0], roll(details[1], 32, 1))
        c2[b, pl.ds(6, 40), :] = jnp.maximum(detail, pc[b, pl.ds(6, 40), :])

    for copy in hx2 + fp:
        copy.wait_recv()
    loop(0, BLK, stage_x2)

    def stage_x3(c):
        rows = []
        for k in range(2):
            low, high = split(s2, (2 * c + k,), 0, 24)
            rows += [low, high, low[:16]]
        turned = jnp.concatenate(rows, axis=0).T
        for g in range(4):
            piece = turned[32 * g : 32 * g + 32]
            t3[c, g, pl.ds(8, 32), :] = piece
            t3_s[c, g, :, :] = piece[30:32]

    loop(0, TWO, stage_x3)
    hy3 = [
        remote(t3.at[:, :, pl.ds(8, 6)], t3.at[:, :, pl.ds(40, 6)], y_prev),
        remote(t3_s, t3_r, y_next),
    ]
    for copy in hy3:
        copy.start()

    def stage_p2(c):
        rows = []
        for k in range(2):
            pooled = pool_rows(c2, (2 * c + k,), 6, 24)
            rows += [pooled, pooled, pooled[:16]]
        p2[c, :, :] = jnp.concatenate(rows, axis=0).T
        for g in range(4):
            pooled = pool_rows(p2, (c,), 32 * g, 16)
            p3[c, g, pl.ds(8, 16), :] = pooled
            f3p_s[0, c, g, :, :] = pooled[0:1]
            f3p_s[1, c, g, :, :] = pooled[15:16]

    loop(0, TWO, stage_p2)
    f3p = frames(f3p_s, f3p_r, y_prev, y_next)
    for copy in f3p:
        copy.start()

    def stage_l2x(c):
        rows = [box_rows(c2, (jnp.minimum(4 * c + k, BLK - 1),), 32) for k in range(4)]
        turned = jnp.concatenate(rows, axis=0).T
        for g in range(4):
            y2[c, g, pl.ds(8, 32), :] = turned[32 * g : 32 * g + 32]
            f2y_s[0, c, g, :, :] = turned[32 * g : 32 * g + 1]
            f2y_s[1, c, g, :, :] = turned[32 * g + 31 : 32 * g + 32]

    loop(0, QUAD, stage_l2x)
    f2y = frames(f2y_s, f2y_r, y_prev, y_next)
    for copy in f2y:
        copy.start()

    for copy in f1x:
        copy.wait_recv()

    def stage_l1x(b):
        for k in range(2):
            e1[b, k, 7:8, :] = f1x_r[0, b, k, :, :]
            e1[b, k, 72:73, :] = f1x_r[1, b, k, :, :]
            eb[b, k, :, :] = box_rows(e1, (b, k), 64)

    def deep(b, k):
        return jnp.maximum(jnp.maximum(eb[b, k], eb[b + 1, k]), eb[b + 2, k])

    def stage_o1(b):
        for k in range(2):
            deepest = deep(b, k)
            o1[b + HALF * k, :, :] = deepest[:, :64]
            if k == 0:
                o1[b + BLK, :, :] = roll(deepest, 64, 1)[:, :64]

    def stage_o1_rest(b):
        o1[b + HALF + BLK, :, :] = roll(deep(b, 1), 64, 1)[:, :64]

    def finish_l1():
        half = lane_ids(64) < 64
        for b in range(2):
            later = roll(eb[b, 1], 64, 1)
            eb[BLK + b, 0] = jnp.where(half, roll(eb[b, 0], 64, 1), later)
            eb[BLK + b, 1] = later
        loop(0, BLK, stage_o1)
        loop(0, OUT - HALF - BLK, stage_o1_rest)

    loop(0, BLK, stage_l1x)
    finish_l1()

    def stage_y3(c):
        rows = []
        for g in range(4):
            t3[c, g, 6:8, :] = t3_r[c, g, :, :]
            p3[c, g, 7:8, :] = f3p_r[0, c, g, :, :]
            p3[c, g, 24:25, :] = f3p_r[1, c, g, :, :]
            low, high = split(t3, (c, g), 6, 24)
            high = jnp.abs(high)
            detail = jnp.maximum(high, roll(jnp.maximum(jnp.abs(low), high), 104, 1))
            c3[c, g, :, :] = jnp.maximum(detail, p3[c, g, pl.ds(7, 24), :])
            boxed = jnp.maximum(c3[c, g, pl.ds(0, 16), :], c3[c, g, pl.ds(1, 16), :])
            rows.append(jnp.maximum(boxed, c3[c, g, pl.ds(2, 16), :]))
        x3[c, :, :] = jnp.concatenate(rows + rows, axis=0).T

    for copy in hy3 + f3p:
        copy.wait_recv()
    loop(0, TWO, stage_y3)

    for copy in f2y:
        copy.wait_recv()

    offsets = (0, HALF, BLK, HALF + BLK)
    for c in range(QUAD):
        rows = []
        for g in range(4):
            y2[c, g, 7:8, :] = f2y_r[0, c, g, :, :]
            y2[c, g, 40:41, :] = f2y_r[1, c, g, :, :]
            rows.append(box_rows(y2, (c, g), 32))
        turned = jnp.concatenate(rows, axis=0).T
        for k in range(min(4, BLK - 4 * c)):
            block = turned[32 * k : 32 * k + 32]
            for g in range(4):
                spun = roll(block, 128 - 32 * g, 1) if g else block
                w2[pl.ds(4 * c + k + offsets[g], 32, stride=PITCH), :] = spun

    def planes_last(w, x, n):
        start = pl.multiple_of(x * PITCH, 8)
        deepest = w[pl.ds(start, 40), :]
        for shift in (1, 2):
            deepest = jnp.maximum(deepest, w[pl.ds(start + shift, 40), :])
        return deepest.T[:n, :OUT]

    def stage_o2(x):
        o2[x, :, :] = planes_last(w2, x, 32)

    loop(0, 32, stage_o2)

    for c in range(TWO):
        for k in range(2):
            block = x3[c, pl.ds(64 * k, 16), :]
            for shift in (1, 2):
                block = jnp.maximum(block, x3[c, pl.ds(64 * k + shift, 16), :])
            for g in range(4):
                spun = roll(block, 128 - 16 * g, 1) if g else block
                w3[pl.ds(2 * c + k + offsets[g], 16, stride=PITCH), :] = spun

    def stage_o3(x):
        o3[x, :, :] = planes_last(w3, x, 16)

    loop(0, 16, stage_o3)

    for row in hx1 + hy1 + [f1y, hx2, fp, f1x, hy3, f3p, f2y]:
        for copy in row:
            copy.wait_send()


def shards(vorticity):
    f32 = jnp.float32
    copies = 5 * len(CHUNKS) + 14
    rows = lambda *shape: pltpu.VMEM(shape, f32)
    pair = lambda *shape: [rows(*shape, 128)] * 2
    o1, o2, o3 = pl.pallas_call(
        kernel,
        out_shape=[
            jax.ShapeDtypeStruct((OUT, 64, 64), f32),
            jax.ShapeDtypeStruct((32, 32, OUT), f32),
            jax.ShapeDtypeStruct((16, 16, OUT), f32),
        ],
        in_specs=[pl.BlockSpec(memory_space=pltpu.HBM)],
        out_specs=[pl.BlockSpec(memory_space=pltpu.VMEM)] * 3,
        scratch_shapes=[
            rows(Z, 136, 128),
            rows(Z, 136, 128),
            rows(HALF, 72, 128),
            rows(HALF, 80, 128),
            rows(BLK, 2, 88, 128),
            rows(BLK, 56, 128),
            rows(BLK, 56, 128),
            rows(BLK, 48, 128),
            rows(5, 128, 128),
            rows(TWO, 4, 64, 128),
            rows(TWO, 128, 128),
            rows(TWO, 4, 32, 128),
            rows(TWO, 4, 24, 128),
            rows(BLK, 2, 80, 128),
            rows(BLK + 2, 2, 64, 128),
            rows(QUAD, 4, 48, 128),
            rows(32 * PITCH, 128),
            rows(TWO, 128, 128),
            rows(16 * PITCH, 128),
            *pair(HALF, 8),
            rows(HALF, 16, 128),
            *pair(2, HALF, 1),
            *pair(2, BLK, 2, 1),
            *pair(2, BLK, 2),
            *pair(2, QUAD, 4, 1),
            *pair(2, TWO, 4, 1),
            *pair(TWO, 4, 2),
            pltpu.SemaphoreType.DMA((2 * len(CHUNKS),)),
            pltpu.SemaphoreType.DMA((copies,)),
            pltpu.SemaphoreType.DMA((copies,)),
        ],
        compiler_params=pltpu.CompilerParams(
            collective_id=0, has_side_effects=True, vmem_limit_bytes=51 * 2**20
        ),
    )(vorticity)
    return o1, jnp.transpose(o2, (2, 0, 1)), jnp.transpose(o3, (2, 0, 1))


def solution(mesh):
    placed = P(None, "gx", "gy")
    return jax.shard_map(
        shards, mesh=mesh, in_specs=(placed,), out_specs=(placed,) * 3, check_vma=False
    )
```

```python
import functools

import jax
import jax.numpy as jnp
from jax import lax
from jax.experimental import pallas as pl
from jax.experimental.pallas import tpu as pltpu
from jax.sharding import PartitionSpec as P

H = (
    0.3326705529509569,
    0.8068915093133388,
    0.4598775021193313,
    -0.13501102001039084,
    -0.08544127388224149,
    0.035226291882100656,
)
G = tuple((-1) ** t * H[5 - t] for t in range(6))
Z = 38
HALF = 20
BLK = 10
QUAD = 3
TWO = 5
STRIPS = 3
HR = 4
OUT = Z - 2
PITCH = 48
UNROLL = 5
CHUNKS = ((0, 10), (10, 20))
MESH = pl.DeviceIdType.MESH
roll = pltpu.roll


def lane_ids(rows):
    return lax.broadcasted_iota(jnp.int32, (rows, 128), 1)


def split(ref, lead, start, n):
    low = high = None
    for t in range(6):
        tap = ref[lead + (pl.ds(start + t, n, stride=2), slice(None))]
        low = tap * H[t] if low is None else low + tap * H[t]
        high = tap * G[t] if high is None else high + tap * G[t]
    return low, high


def pool_rows(ref, lead, start, n):
    return jnp.maximum(
        ref[lead + (pl.ds(start, n, stride=2), slice(None))],
        ref[lead + (pl.ds(start + 1, n, stride=2), slice(None))],
    )


def box_rows(ref, lead, n):
    return jnp.maximum(
        jnp.maximum(
            ref[lead + (pl.ds(7, n), slice(None))],
            ref[lead + (pl.ds(9, n), slice(None))],
        ),
        ref[lead + (pl.ds(8, n), slice(None))],
    )


def pair_of(q):
    return jnp.minimum(q + HALF, Z - 1)


def loop(lo, hi, body):
    def step(i, _):
        body(i)
        return 0

    lax.fori_loop(lo, hi, step, 0, unroll=min(UNROLL, hi - lo))


def kernel(
    v, o1, o2, o3,
    vb, tb, s1, d1, t2, s2, c2, pc, p1, t3, p2, p3, c3, e1, eb, y2, w2, x3, w3,
    lk_s, lk_r, lh, f1y_s, f1y_r, f1x_s, f1x_r, fp_s, fp_r, sl, us, ts, ss, ds, ta, tx,
    f2y_s, f2y_r, f3p_s, f3p_r, t3_s, t3_r,
    in_sem, send_sem, recv_sem,
):
    nx, ny = lax.axis_size("gx"), lax.axis_size("gy")
    ix, iy = lax.axis_index("gx"), lax.axis_index("gy")
    x_prev = (lax.rem(ix + nx - 1, nx), iy)
    x_next = (lax.rem(ix + 1, nx), iy)
    y_prev = (ix, lax.rem(iy + ny - 1, ny))
    y_next = (ix, lax.rem(iy + 1, ny))
    counter = [0]

    def remote(src, dst, target):
        k = counter[0]
        counter[0] += 1
        return pltpu.make_async_remote_copy(
            src_ref=src, dst_ref=dst, send_sem=send_sem.at[k], recv_sem=recv_sem.at[k],
            device_id=target, device_id_type=MESH,
        )

    def frames(send, recv, prev, following):
        return [
            remote(send.at[0], recv.at[1], prev),
            remote(send.at[1], recv.at[0], following),
        ]

    spans = []
    for q0, q1 in CHUNKS:
        spans.append(((q0, q1), (q0 + HALF, min(q1 + HALF, Z))))
    loads, hx1, hy1 = [], [], []
    for number, pieces in enumerate(spans):
        row = []
        for part, (a, b) in enumerate(pieces):
            row.append(
                pltpu.make_async_copy(
                    v.at[pl.ds(a, b - a)], vb.at[pl.ds(a, b - a), pl.ds(0, 128)],
                    in_sem.at[2 * number + part],
                )
            )
        loads.append(row)
    for row in loads:
        for copy in row:
            copy.start()
    edge = pltpu.make_async_copy(
        v.at[:, pl.ds(0, 8)], sl.at[:, pl.ds(8, 8)], in_sem.at[2 * len(CHUNKS)]
    )
    edge.start()

    barrier = pltpu.get_barrier_semaphore()
    for device in (x_prev, x_next, y_prev, y_next):
        pl.semaphore_signal(barrier, inc=1, device_id=device, device_id_type=MESH)
    pl.semaphore_wait(barrier, 4)

    for pieces in spans:
        row = [
            remote(
                v.at[pl.ds(a, b - a), pl.ds(0, HR)],
                vb.at[pl.ds(a, b - a), pl.ds(128, HR)], x_prev,
            )
            for a, b in pieces
        ]
        for copy in row:
            copy.start()
        hx1.append(row)
    hs1 = remote(v.at[:, pl.ds(120, 8)], sl.at[:, pl.ds(0, 8)], x_next)
    hs1.start()

    def stage_x1(p):
        lows, highs = [], []
        for piece in range(2):
            low, high = split(vb, (p,), 64 * piece, 32)
            lows.append(low)
            highs.append(high)
        tb[p, pl.ds(0, 128), :] = jnp.concatenate(lows + highs, axis=0).T

    def both(ref, q, start, n):
        later = roll(ref[pair_of(q), pl.ds(start, n), :], 64, 1)
        return jnp.where(lane_ids(n) < 64, ref[q, pl.ds(start, n), :], later)

    def stage_k1(q):
        lk_s[q, :, :] = both(tb, q, HR, 8)

    for number, pieces in enumerate(spans):
        for copy in loads[number]:
            copy.wait()
        for copy in hx1[number]:
            copy.wait_recv()
        for a, b in pieces:
            loop(a, b, stage_x1)
        row = [
            remote(
                tb.at[pl.ds(a, b - a), pl.ds(0, HR)],
                tb.at[pl.ds(a, b - a), pl.ds(128, HR)], y_prev,
            )
            for a, b in pieces
        ]
        for copy in row:
            copy.start()
        q0, q1 = CHUNKS[number]
        loop(q0, q1, stage_k1)
        copy = remote(lk_s.at[pl.ds(q0, q1 - q0)], lk_r.at[pl.ds(q0, q1 - q0)], y_prev)
        copy.start()
        hy1.append(row + [copy])

    def stage_xs(p):
        low, high = split(sl, (jnp.minimum(p, Z - 1),), 0, 4)
        us[p, 0:4, :] = low
        us[p, 4:8, :] = high

    def stage_ts(i):
        ts[i, pl.ds(8, 128), :] = us[pl.ds(16 * i, 16)].reshape(128, 128).T

    edge.wait()
    hs1.wait_recv()
    loop(0, 16 * STRIPS, stage_xs)
    loop(0, STRIPS, stage_ts)
    hs2 = [
        remote(ts.at[:, pl.ds(8, 16)], ts.at[:, pl.ds(136, 16)], y_prev),
        remote(ts.at[:, pl.ds(128, 8)], ts.at[:, pl.ds(0, 8)], y_next),
    ]
    for copy in hs2:
        copy.start()

    def stage_ys(i):
        low, high = split(ts, (i,), 6, 70)
        high = jnp.abs(high)
        ss[i, pl.ds(7, 70), :] = low
        ds[i, pl.ds(7, 70), :] = jnp.maximum(
            high, roll(jnp.maximum(jnp.abs(low), high), 124, 1)
        )

    def stage_zs(i):
        low, high = split(ss, (i,), 8, 32)
        pooled = pool_rows(ds, (i,), 8, 32)
        turned = jnp.concatenate([low, high, pooled, pooled], axis=0).T
        ta[pl.ds(16 * i, 16)] = turned.reshape(16, 8, 128)
        boxed = box_rows(ds, (i,), 64)
        turned = jnp.concatenate([boxed, boxed], axis=0).T
        tx[pl.ds(16 * i, 16)] = turned.reshape(16, 8, 128)

    def stage_left(b):
        four, two = lane_ids(4), lane_ids(2)
        pooled = []
        for k in range(2):
            p = b + HALF * k
            t2[b, k, 4:8, :] = jnp.where(
                four < 64, ta[p, 0:4, :], roll(ta[p + BLK, 0:4, :], 64, 1)
            )
            e1[b, k, 7:8, :] = jnp.where(
                lane_ids(1) < 64, tx[p, 3:4, :], tx[p + BLK, 3:4, :]
            )
        for p in (b, b + HALF, b + BLK, b + HALF + BLK):
            pooled.append(pool_rows(ta, (p,), 0, 2))
        lower = roll(jnp.where(two < 96, pooled[0], pooled[1]), 64, 1)
        upper = jnp.where(two < 96, pooled[2], pooled[3])
        pc[b, 6:8, :] = jnp.where(two < 64, lower, upper)

    first = lane_ids(32) < 64

    def stage_y1(q):
        other = pair_of(q)
        for piece in range(2):
            low_a, high_a = split(tb, (q,), 64 * piece, 32)
            low_b, high_b = split(tb, (other,), 64 * piece, 32)
            turned_a, turned_b = roll(low_a, 64, 1), roll(low_b, 64, 1)
            s1[q, pl.ds(32 * piece, 32), :] = jnp.where(first, low_a, turned_b)
            cross = jnp.abs(jnp.where(first, turned_a, low_b))
            high_a, high_b = jnp.abs(high_a), jnp.abs(high_b)
            high_a = jnp.maximum(high_a, roll(high_a, 64, 1))
            high_b = jnp.maximum(high_b, roll(high_b, 64, 1))
            detail = jnp.maximum(jnp.where(first, high_a, high_b), cross)
            d1[q, pl.ds(8 + 32 * piece, 32), :] = detail
            if piece == 0:
                f1y_s[0, q, :, :] = detail[0:1]
            else:
                f1y_s[1, q, :, :] = detail[31:32]

    def stage_k2(q):
        lh[q, pl.ds(0, HR), :] = both(tb, q, 128, HR)
        lh[q, pl.ds(HR, 8), :] = lk_r[q, :, :]
        low = None
        for t in range(6):
            tap = lh[q, pl.ds(t, HR, stride=2), :] * H[t]
            low = tap if low is None else low + tap
        s1[q, pl.ds(64, HR), :] = low

    for number, (q0, q1) in enumerate(CHUNKS):
        for copy in hy1[number]:
            copy.wait_recv()
        loop(q0, q1, stage_y1)
        loop(q0, q1, stage_k2)
    f1y = frames(f1y_s, f1y_r, y_prev, y_next)
    for copy in f1y:
        copy.start()

    quarter = lax.rem(lane_ids(32), 64) < 32

    def stage_p1(b):
        rows = [pool_rows(d1, (b + 5 * k,), 8, 32) for k in range(4)]
        p1[b, :, :] = jnp.concatenate(rows, axis=0).T
        pool_a = pool_rows(p1, (b,), 0, 32)
        pool_b = pool_rows(p1, (b,), 64, 32)
        for block, pooled in (
            (b, jnp.where(quarter, pool_a, roll(pool_b, 32, 1))),
            (b + 5, jnp.where(quarter, roll(pool_a, 96, 1), pool_b)),
        ):
            pc[block, pl.ds(8, 32), :] = pooled
            fp_s[block, :, :] = pooled[0:2]

    def stage_y2(b):
        rows = []
        for q in (b, b + BLK):
            rows += split(s1, (q,), 0, 32)
        turned = jnp.concatenate(rows, axis=0).T
        t2[b, 0, pl.ds(8, 64), :] = turned[:64]
        t2[b, 1, pl.ds(8, 64), :] = turned[64:]

    loop(0, BLK, stage_y2)
    hx2 = [remote(t2.at[:, :, pl.ds(8, 16)], t2.at[:, :, pl.ds(72, 16)], x_prev)]
    for copy in hx2:
        copy.start()
    loop(0, 5, stage_p1)
    fp = [remote(fp_s, fp_r, x_prev)]
    for copy in fp:
        copy.start()

    for copy in f1y:
        copy.wait_recv()

    def stage_l1y(b):
        rows = []
        for q in (b, b + BLK):
            d1[q, 7:8, :] = f1y_r[0, q, :, :]
            d1[q, 72:73, :] = f1y_r[1, q, :, :]
            rows.append(box_rows(d1, (q,), 64))
        turned = jnp.concatenate(rows, axis=0).T
        for k in range(2):
            e1[b, k, pl.ds(8, 64), :] = turned[64 * k : 64 * k + 64]
            f1x_s[b, k, :, :] = turned[64 * k : 64 * k + 1]

    loop(0, BLK, stage_l1y)
    f1x = [remote(f1x_s, f1x_r, x_prev)]
    for copy in f1x:
        copy.start()

    for copy in hs2:
        copy.wait_recv()
    loop(0, STRIPS, stage_ys)
    loop(0, STRIPS, stage_zs)
    loop(0, BLK, stage_left)

    wide = lax.rem(lane_ids(40), 64) < 32

    def stage_x2(b):
        pc[b, 40:42, :] = fp_r[b, :, :]
        lows, details = [], []
        for k in range(2):
            low, high = split(t2, (b, k), 4, 40)
            high = jnp.abs(high)
            lows.append(low)
            details.append(
                jnp.maximum(high, roll(jnp.maximum(jnp.abs(low), high), 96, 1))
            )
        s2[b, pl.ds(0, 40), :] = jnp.where(wide, lows[0], roll(lows[1], 32, 1))
        detail = jnp.where(wide, details[0], roll(details[1], 32, 1))
        c2[b, pl.ds(6, 40), :] = jnp.maximum(detail, pc[b, pl.ds(6, 40), :])

    for copy in hx2 + fp:
        copy.wait_recv()
    loop(0, BLK, stage_x2)

    def stage_x3(c):
        rows = []
        for k in range(2):
            low, high = split(s2, (2 * c + k,), 0, 24)
            rows += [low, high, low[:16]]
        turned = jnp.concatenate(rows, axis=0).T
        for g in range(4):
            piece = turned[32 * g : 32 * g + 32]
            t3[c, g, pl.ds(8, 32), :] = piece
            t3_s[c, g, :, :] = piece[30:32]

    loop(0, TWO, stage_x3)
    hy3 = [
        remote(t3.at[:, :, pl.ds(8, 6)], t3.at[:, :, pl.ds(40, 6)], y_prev),
        remote(t3_s, t3_r, y_next),
    ]
    for copy in hy3:
        copy.start()

    def stage_p2(c):
        rows = []
        for k in range(2):
            pooled = pool_rows(c2, (2 * c + k,), 6, 24)
            rows += [pooled, pooled, pooled[:16]]
        p2[c, :, :] = jnp.concatenate(rows, axis=0).T
        for g in range(4):
            pooled = pool_rows(p2, (c,), 32 * g, 16)
            p3[c, g, pl.ds(8, 16), :] = pooled
            f3p_s[0, c, g, :, :] = pooled[0:1]
            f3p_s[1, c, g, :, :] = pooled[15:16]

    loop(0, TWO, stage_p2)
    f3p = frames(f3p_s, f3p_r, y_prev, y_next)
    for copy in f3p:
        copy.start()

    def stage_l2x(c):
        rows = [box_rows(c2, (jnp.minimum(4 * c + k, BLK - 1),), 32) for k in range(4)]
        turned = jnp.concatenate(rows, axis=0).T
        for g in range(4):
            y2[c, g, pl.ds(8, 32), :] = turned[32 * g : 32 * g + 32]
            f2y_s[0, c, g, :, :] = turned[32 * g : 32 * g + 1]
            f2y_s[1, c, g, :, :] = turned[32 * g + 31 : 32 * g + 32]

    loop(0, QUAD, stage_l2x)
    f2y = frames(f2y_s, f2y_r, y_prev, y_next)
    for copy in f2y:
        copy.start()

    for copy in f1x:
        copy.wait_recv()

    def stage_l1x(b):
        for k in range(2):
            e1[b, k, 72:73, :] = f1x_r[b, k, :, :]
            eb[b, k, :, :] = box_rows(e1, (b, k), 64)

    def deep(b, k):
        return jnp.maximum(jnp.maximum(eb[b, k], eb[b + 1, k]), eb[b + 2, k])

    def stage_o1(b):
        for k in range(2):
            deepest = deep(b, k)
            o1[b + HALF * k, :, :] = deepest[:, :64]
            if k == 0:
                o1[b + BLK, :, :] = roll(deepest, 64, 1)[:, :64]

    def stage_o1_rest(b):
        o1[b + HALF + BLK, :, :] = roll(deep(b, 1), 64, 1)[:, :64]

    def finish_l1():
        half = lane_ids(64) < 64
        for b in range(2):
            later = roll(eb[b, 1], 64, 1)
            eb[BLK + b, 0] = jnp.where(half, roll(eb[b, 0], 64, 1), later)
            eb[BLK + b, 1] = later
        loop(0, BLK, stage_o1)
        loop(0, OUT - HALF - BLK, stage_o1_rest)

    loop(0, BLK, stage_l1x)
    finish_l1()

    def stage_y3(c):
        rows = []
        for g in range(4):
            t3[c, g, 6:8, :] = t3_r[c, g, :, :]
            p3[c, g, 7:8, :] = f3p_r[0, c, g, :, :]
            p3[c, g, 24:25, :] = f3p_r[1, c, g, :, :]
            low, high = split(t3, (c, g), 6, 24)
            high = jnp.abs(high)
            detail = jnp.maximum(high, roll(jnp.maximum(jnp.abs(low), high), 104, 1))
            c3[c, g, :, :] = jnp.maximum(detail, p3[c, g, pl.ds(7, 24), :])
            boxed = jnp.maximum(c3[c, g, pl.ds(0, 16), :], c3[c, g, pl.ds(1, 16), :])
            rows.append(jnp.maximum(boxed, c3[c, g, pl.ds(2, 16), :]))
        x3[c, :, :] = jnp.concatenate(rows + rows, axis=0).T

    for copy in hy3 + f3p:
        copy.wait_recv()
    loop(0, TWO, stage_y3)

    for copy in f2y:
        copy.wait_recv()

    offsets = (0, HALF, BLK, HALF + BLK)
    for c in range(QUAD):
        rows = []
        for g in range(4):
            y2[c, g, 7:8, :] = f2y_r[0, c, g, :, :]
            y2[c, g, 40:41, :] = f2y_r[1, c, g, :, :]
            rows.append(box_rows(y2, (c, g), 32))
        turned = jnp.concatenate(rows, axis=0).T
        for k in range(min(4, BLK - 4 * c)):
            block = turned[32 * k : 32 * k + 32]
            for g in range(4):
                spun = roll(block, 128 - 32 * g, 1) if g else block
                w2[pl.ds(4 * c + k + offsets[g], 32, stride=PITCH), :] = spun

    def planes_last(w, x, n):
        start = pl.multiple_of(x * PITCH, 8)
        deepest = w[pl.ds(start, 40), :]
        for shift in (1, 2):
            deepest = jnp.maximum(deepest, w[pl.ds(start + shift, 40), :])
        return deepest.T[:n, :OUT]

    def stage_o2(x):
        o2[x, :, :] = planes_last(w2, x, 32)

    loop(0, 32, stage_o2)

    for c in range(TWO):
        for k in range(2):
            block = x3[c, pl.ds(64 * k, 16), :]
            for shift in (1, 2):
                block = jnp.maximum(block, x3[c, pl.ds(64 * k + shift, 16), :])
            for g in range(4):
                spun = roll(block, 128 - 16 * g, 1) if g else block
                w3[pl.ds(2 * c + k + offsets[g], 16, stride=PITCH), :] = spun

    def stage_o3(x):
        o3[x, :, :] = planes_last(w3, x, 16)

    loop(0, 16, stage_o3)

    for row in hx1 + hy1 + [[hs1], hs2, f1y, hx2, fp, f1x, hy3, f3p, f2y]:
        for copy in row:
            copy.wait_send()


def write_out(a1, a2, a3, b1, b2, b3, sems):
    copies = [
        pltpu.make_async_copy(src, dst, sems.at[k])
        for k, (src, dst) in enumerate(((a1, b1), (a2, b2), (a3, b3)))
    ]
    for copy in copies:
        copy.start()
    for copy in copies:
        copy.wait()


def shards(vorticity):
    f32 = jnp.float32
    copies = 5 * len(CHUNKS) + 14
    rows = lambda *shape: pltpu.VMEM(shape, f32)
    pair = lambda *shape: [rows(*shape, 128)] * 2
    results = [
        jax.ShapeDtypeStruct((OUT, 64, 64), f32),
        jax.ShapeDtypeStruct((32, 32, OUT), f32),
        jax.ShapeDtypeStruct((16, 16, OUT), f32),
    ]
    inner = pl.pallas_call(
        kernel,
        out_shape=results,
        in_specs=[pl.BlockSpec(memory_space=pltpu.HBM)],
        out_specs=[pl.BlockSpec(memory_space=pltpu.VMEM)] * 3,
        scratch_shapes=[
            rows(Z, 136, 128),
            rows(Z, 136, 128),
            rows(HALF, 72, 128),
            rows(HALF, 80, 128),
            rows(BLK, 2, 88, 128),
            rows(BLK, 56, 128),
            rows(BLK, 56, 128),
            rows(BLK, 48, 128),
            rows(5, 128, 128),
            rows(TWO, 4, 64, 128),
            rows(TWO, 128, 128),
            rows(TWO, 4, 32, 128),
            rows(TWO, 4, 24, 128),
            rows(BLK, 2, 80, 128),
            rows(BLK + 2, 2, 64, 128),
            rows(QUAD, 4, 48, 128),
            rows(32 * PITCH, 128),
            rows(TWO, 128, 128),
            rows(16 * PITCH, 128),
            *pair(HALF, 8),
            rows(HALF, 16, 128),
            *pair(2, HALF, 1),
            *pair(BLK, 2, 1),
            *pair(BLK, 2),
            rows(Z, 16, 128),
            rows(16 * STRIPS, 8, 128),
            rows(STRIPS, 152, 128),
            rows(STRIPS, 80, 128),
            rows(STRIPS, 80, 128),
            rows(16 * STRIPS, 8, 128),
            rows(16 * STRIPS, 8, 128),
            *pair(2, QUAD, 4, 1),
            *pair(2, TWO, 4, 1),
            *pair(TWO, 4, 2),
            pltpu.SemaphoreType.DMA((2 * len(CHUNKS) + 1,)),
            pltpu.SemaphoreType.DMA((copies,)),
            pltpu.SemaphoreType.DMA((copies,)),
        ],
        compiler_params=pltpu.CompilerParams(
            collective_id=0, has_side_effects=True, vmem_limit_bytes=51 * 2**20
        ),
    )(vorticity)
    o1, o2, o3 = pl.pallas_call(
        write_out,
        out_shape=results,
        in_specs=[pl.BlockSpec(memory_space=pl.ANY)] * 3,
        out_specs=[pl.BlockSpec(memory_space=pl.ANY)] * 3,
        scratch_shapes=[pltpu.SemaphoreType.DMA((3,))],
        compiler_params=pltpu.CompilerParams(vmem_limit_bytes=2**20),
    )(*inner)
    return o1, jnp.transpose(o2, (2, 0, 1)), jnp.transpose(o3, (2, 0, 1))


def solution(mesh):
    placed = P(None, "gx", "gy")
    return jax.shard_map(
        shards, mesh=mesh, in_specs=(placed,), out_specs=(placed,) * 3, check_vma=False
    )
```

```python
import functools

import jax
import jax.numpy as jnp
from jax import lax
from jax.experimental import pallas as pl
from jax.experimental.pallas import tpu as pltpu
from jax.sharding import PartitionSpec as P

H = (
    0.3326705529509569,
    0.8068915093133388,
    0.4598775021193313,
    -0.13501102001039084,
    -0.08544127388224149,
    0.035226291882100656,
)
G = tuple((-1) ** t * H[5 - t] for t in range(6))
Z = 38
HALF = 20
BLK = 10
QUAD = 3
TWO = 5
STRIPS = 3
HR = 4
OUT = Z - 2
PITCH = 48
UNROLL = 5
CHUNKS = ((0, 10), (10, 20))
MESH = pl.DeviceIdType.MESH
roll = pltpu.roll


def lane_ids(rows):
    return lax.broadcasted_iota(jnp.int32, (rows, 128), 1)


def split(ref, lead, start, n):
    low = high = None
    for t in range(6):
        tap = ref[lead + (pl.ds(start + t, n, stride=2), slice(None))]
        low = tap * H[t] if low is None else low + tap * H[t]
        high = tap * G[t] if high is None else high + tap * G[t]
    return low, high


def pool_rows(ref, lead, start, n):
    return jnp.maximum(
        ref[lead + (pl.ds(start, n, stride=2), slice(None))],
        ref[lead + (pl.ds(start + 1, n, stride=2), slice(None))],
    )


def box_rows(ref, lead, n):
    return jnp.maximum(
        jnp.maximum(
            ref[lead + (pl.ds(7, n), slice(None))],
            ref[lead + (pl.ds(9, n), slice(None))],
        ),
        ref[lead + (pl.ds(8, n), slice(None))],
    )


def pair_of(q):
    return jnp.minimum(q + HALF, Z - 1)


def loop(lo, hi, body):
    def step(i, _):
        body(i)
        return 0

    lax.fori_loop(lo, hi, step, 0, unroll=min(UNROLL, hi - lo))


def kernel(
    v, o1, o2, o3,
    vb, tb, s1, d1, t2, s2, c2, pc, p1, t3, p2, p3, c3, e1, eb, y2, w2, x3, w3,
    lk_s, lk_r, lh, f1y_s, f1y_r, f1x_s, f1x_r, fp_s, fp_r, sl, us, ts, ss, ds, ta, tx,
    f2y_s, f2y_r, f3p_s, f3p_r, t3_s, t3_r,
    in_sem, send_sem, recv_sem,
):
    nx, ny = lax.axis_size("gx"), lax.axis_size("gy")
    ix, iy = lax.axis_index("gx"), lax.axis_index("gy")
    x_prev = (lax.rem(ix + nx - 1, nx), iy)
    x_next = (lax.rem(ix + 1, nx), iy)
    y_prev = (ix, lax.rem(iy + ny - 1, ny))
    y_next = (ix, lax.rem(iy + 1, ny))
    counter = [0]

    def remote(src, dst, target):
        k = counter[0]
        counter[0] += 1
        return pltpu.make_async_remote_copy(
            src_ref=src, dst_ref=dst, send_sem=send_sem.at[k], recv_sem=recv_sem.at[k],
            device_id=target, device_id_type=MESH,
        )

    def frames(send, recv, prev, following):
        return [
            remote(send.at[0], recv.at[1], prev),
            remote(send.at[1], recv.at[0], following),
        ]

    spans = []
    for q0, q1 in CHUNKS:
        spans.append(((q0, q1), (q0 + HALF, min(q1 + HALF, Z))))
    loads, hx1, hy1 = [], [], []
    for number, pieces in enumerate(spans):
        row = []
        for part, (a, b) in enumerate(pieces):
            row.append(
                pltpu.make_async_copy(
                    v.at[pl.ds(a, b - a)], vb.at[pl.ds(a, b - a), pl.ds(0, 128)],
                    in_sem.at[2 * number + part],
                )
            )
        loads.append(row)
    for row in loads:
        for copy in row:
            copy.start()
    edge = pltpu.make_async_copy(
        v.at[:, pl.ds(0, 8)], sl.at[:, pl.ds(8, 8)], in_sem.at[2 * len(CHUNKS)]
    )
    edge.start()

    barrier = pltpu.get_barrier_semaphore()
    for device in (x_prev, x_next, y_prev, y_next):
        pl.semaphore_signal(barrier, inc=1, device_id=device, device_id_type=MESH)

    for pieces in spans:
        hx1.append([
            remote(
                v.at[pl.ds(a, b - a), pl.ds(0, HR)],
                vb.at[pl.ds(a, b - a), pl.ds(128, HR)], x_prev,
            )
            for a, b in pieces
        ])
    hs1 = remote(v.at[:, pl.ds(120, 8)], sl.at[:, pl.ds(0, 8)], x_next)
    for (q0, q1), pieces in zip(CHUNKS, spans):
        row = [
            remote(
                tb.at[pl.ds(a, b - a), pl.ds(0, HR)],
                tb.at[pl.ds(a, b - a), pl.ds(128, HR)], y_prev,
            )
            for a, b in pieces
        ]
        row.append(
            remote(lk_s.at[pl.ds(q0, q1 - q0)], lk_r.at[pl.ds(q0, q1 - q0)], y_prev)
        )
        hy1.append(row)

    def stage_x1(p):
        lows, highs = [], []
        for piece in range(2):
            low, high = split(vb, (p,), 64 * piece, 32)
            lows.append(low)
            highs.append(high)
        tb[p, pl.ds(0, 128), :] = jnp.concatenate(lows + highs, axis=0).T

    def both(ref, q, start, n):
        later = roll(ref[pair_of(q), pl.ds(start, n), :], 64, 1)
        return jnp.where(lane_ids(n) < 64, ref[q, pl.ds(start, n), :], later)

    def stage_k1(q):
        lk_s[q, :, :] = both(tb, q, HR, 8)

    def begin(number):
        for copy in loads[number]:
            copy.wait()
        for copy in hx1[number]:
            copy.wait_recv()
        for a, b in spans[number]:
            loop(a, b, stage_x1)
        loop(*CHUNKS[number], stage_k1)

    def send(number):
        for copy in hy1[number]:
            copy.start()

    even = lax.rem(ix, 2) == 0

    @pl.when(even)
    def _():
        for number in range(len(CHUNKS)):
            begin(number)

    pl.semaphore_wait(barrier, 4)

    hs1.start()
    for row in hx1:
        for copy in row:
            copy.start()

    @pl.when(even)
    def _():
        for number in range(len(CHUNKS)):
            send(number)

    @pl.when(jnp.logical_not(even))
    def _():
        for number in range(len(CHUNKS)):
            begin(number)
            send(number)

    def stage_xs(p):
        low, high = split(sl, (jnp.minimum(p, Z - 1),), 0, 4)
        us[p, 0:4, :] = low
        us[p, 4:8, :] = high

    def stage_ts(i):
        ts[i, pl.ds(8, 128), :] = us[pl.ds(16 * i, 16)].reshape(128, 128).T

    edge.wait()
    hs1.wait_recv()
    loop(0, 16 * STRIPS, stage_xs)
    loop(0, STRIPS, stage_ts)
    hs2 = [
        remote(ts.at[:, pl.ds(8, 16)], ts.at[:, pl.ds(136, 16)], y_prev),
        remote(ts.at[:, pl.ds(128, 8)], ts.at[:, pl.ds(0, 8)], y_next),
    ]
    for copy in hs2:
        copy.start()

    def stage_ys(i):
        low, high = split(ts, (i,), 6, 70)
        high = jnp.abs(high)
        ss[i, pl.ds(7, 70), :] = low
        ds[i, pl.ds(7, 70), :] = jnp.maximum(
            high, roll(jnp.maximum(jnp.abs(low), high), 124, 1)
        )

    def stage_zs(i):
        low, high = split(ss, (i,), 8, 32)
        pooled = pool_rows(ds, (i,), 8, 32)
        turned = jnp.concatenate([low, high, pooled, pooled], axis=0).T
        ta[pl.ds(16 * i, 16)] = turned.reshape(16, 8, 128)
        boxed = box_rows(ds, (i,), 64)
        turned = jnp.concatenate([boxed, boxed], axis=0).T
        tx[pl.ds(16 * i, 16)] = turned.reshape(16, 8, 128)

    def stage_left(b):
        four, two = lane_ids(4), lane_ids(2)
        pooled = []
        for k in range(2):
            p = b + HALF * k
            t2[b, k, 4:8, :] = jnp.where(
                four < 64, ta[p, 0:4, :], roll(ta[p + BLK, 0:4, :], 64, 1)
            )
            e1[b, k, 7:8, :] = jnp.where(
                lane_ids(1) < 64, tx[p, 3:4, :], tx[p + BLK, 3:4, :]
            )
        for p in (b, b + HALF, b + BLK, b + HALF + BLK):
            pooled.append(pool_rows(ta, (p,), 0, 2))
        lower = roll(jnp.where(two < 96, pooled[0], pooled[1]), 64, 1)
        upper = jnp.where(two < 96, pooled[2], pooled[3])
        pc[b, 6:8, :] = jnp.where(two < 64, lower, upper)

    first = lane_ids(32) < 64

    def stage_y1(q):
        other = pair_of(q)
        for piece in range(2):
            low_a, high_a = split(tb, (q,), 64 * piece, 32)
            low_b, high_b = split(tb, (other,), 64 * piece, 32)
            turned_a, turned_b = roll(low_a, 64, 1), roll(low_b, 64, 1)
            s1[q, pl.ds(32 * piece, 32), :] = jnp.where(first, low_a, turned_b)
            cross = jnp.abs(jnp.where(first, turned_a, low_b))
            high_a, high_b = jnp.abs(high_a), jnp.abs(high_b)
            high_a = jnp.maximum(high_a, roll(high_a, 64, 1))
            high_b = jnp.maximum(high_b, roll(high_b, 64, 1))
            detail = jnp.maximum(jnp.where(first, high_a, high_b), cross)
            d1[q, pl.ds(8 + 32 * piece, 32), :] = detail
            if piece == 0:
                f1y_s[0, q, :, :] = detail[0:1]
            else:
                f1y_s[1, q, :, :] = detail[31:32]

    def stage_k2(q):
        lh[q, pl.ds(0, HR), :] = both(tb, q, 128, HR)
        lh[q, pl.ds(HR, 8), :] = lk_r[q, :, :]
        low = None
        for t in range(6):
            tap = lh[q, pl.ds(t, HR, stride=2), :] * H[t]
            low = tap if low is None else low + tap
        s1[q, pl.ds(64, HR), :] = low

    for number, (q0, q1) in enumerate(CHUNKS):
        for copy in hy1[number]:
            copy.wait_recv()
        loop(q0, q1, stage_y1)
        loop(q0, q1, stage_k2)
    f1y = frames(f1y_s, f1y_r, y_prev, y_next)
    for copy in f1y:
        copy.start()

    quarter = lax.rem(lane_ids(32), 64) < 32

    def stage_p1(b):
        rows = [pool_rows(d1, (b + 5 * k,), 8, 32) for k in range(4)]
        p1[b, :, :] = jnp.concatenate(rows, axis=0).T
        pool_a = pool_rows(p1, (b,), 0, 32)
        pool_b = pool_rows(p1, (b,), 64, 32)
        for block, pooled in (
            (b, jnp.where(quarter, pool_a, roll(pool_b, 32, 1))),
            (b + 5, jnp.where(quarter, roll(pool_a, 96, 1), pool_b)),
        ):
            pc[block, pl.ds(8, 32), :] = pooled
            fp_s[block, :, :] = pooled[0:2]

    def stage_y2(b):
        rows = []
        for q in (b, b + BLK):
            rows += split(s1, (q,), 0, 32)
        turned = jnp.concatenate(rows, axis=0).T
        t2[b, 0, pl.ds(8, 64), :] = turned[:64]
        t2[b, 1, pl.ds(8, 64), :] = turned[64:]

    loop(0, BLK, stage_y2)
    hx2 = [remote(t2.at[:, :, pl.ds(8, 16)], t2.at[:, :, pl.ds(72, 16)], x_prev)]
    for copy in hx2:
        copy.start()
    loop(0, 5, stage_p1)
    fp = [remote(fp_s, fp_r, x_prev)]
    for copy in fp:
        copy.start()

    for copy in hs2:
        copy.wait_recv()
    loop(0, STRIPS, stage_ys)
    loop(0, STRIPS, stage_zs)
    loop(0, BLK, stage_left)

    wide = lax.rem(lane_ids(40), 64) < 32

    def stage_x2(b):
        pc[b, 40:42, :] = fp_r[b, :, :]
        lows, details = [], []
        for k in range(2):
            low, high = split(t2, (b, k), 4, 40)
            high = jnp.abs(high)
            lows.append(low)
            details.append(
                jnp.maximum(high, roll(jnp.maximum(jnp.abs(low), high), 96, 1))
            )
        s2[b, pl.ds(0, 40), :] = jnp.where(wide, lows[0], roll(lows[1], 32, 1))
        detail = jnp.where(wide, details[0], roll(details[1], 32, 1))
        c2[b, pl.ds(6, 40), :] = jnp.maximum(detail, pc[b, pl.ds(6, 40), :])

    for copy in hx2 + fp:
        copy.wait_recv()
    loop(0, BLK, stage_x2)

    def stage_x3(c):
        rows = []
        for k in range(2):
            low, high = split(s2, (2 * c + k,), 0, 24)
            rows += [low, high, low[:16]]
        turned = jnp.concatenate(rows, axis=0).T
        for g in range(4):
            piece = turned[32 * g : 32 * g + 32]
            t3[c, g, pl.ds(8, 32), :] = piece
            t3_s[c, g, :, :] = piece[30:32]

    loop(0, TWO, stage_x3)
    hy3 = [
        remote(t3.at[:, :, pl.ds(8, 6)], t3.at[:, :, pl.ds(40, 6)], y_prev),
        remote(t3_s, t3_r, y_next),
    ]
    for copy in hy3:
        copy.start()

    def stage_p2(c):
        rows = []
        for k in range(2):
            pooled = pool_rows(c2, (2 * c + k,), 6, 24)
            rows += [pooled, pooled, pooled[:16]]
        p2[c, :, :] = jnp.concatenate(rows, axis=0).T
        for g in range(4):
            pooled = pool_rows(p2, (c,), 32 * g, 16)
            p3[c, g, pl.ds(8, 16), :] = pooled
            f3p_s[0, c, g, :, :] = pooled[0:1]
            f3p_s[1, c, g, :, :] = pooled[15:16]

    loop(0, TWO, stage_p2)
    f3p = frames(f3p_s, f3p_r, y_prev, y_next)
    for copy in f3p:
        copy.start()

    def stage_l2x(c):
        rows = [box_rows(c2, (jnp.minimum(4 * c + k, BLK - 1),), 32) for k in range(4)]
        turned = jnp.concatenate(rows, axis=0).T
        for g in range(4):
            y2[c, g, pl.ds(8, 32), :] = turned[32 * g : 32 * g + 32]
            f2y_s[0, c, g, :, :] = turned[32 * g : 32 * g + 1]
            f2y_s[1, c, g, :, :] = turned[32 * g + 31 : 32 * g + 32]

    loop(0, QUAD, stage_l2x)
    f2y = frames(f2y_s, f2y_r, y_prev, y_next)
    for copy in f2y:
        copy.start()

    for copy in f1y:
        copy.wait_recv()

    def stage_l1y(b):
        rows = []
        for q in (b, b + BLK):
            d1[q, 7:8, :] = f1y_r[0, q, :, :]
            d1[q, 72:73, :] = f1y_r[1, q, :, :]
            rows.append(box_rows(d1, (q,), 64))
        turned = jnp.concatenate(rows, axis=0).T
        for k in range(2):
            e1[b, k, pl.ds(8, 64), :] = turned[64 * k : 64 * k + 64]
            f1x_s[b, k, :, :] = turned[64 * k : 64 * k + 1]

    loop(0, BLK, stage_l1y)
    f1x = [remote(f1x_s, f1x_r, x_prev)]
    for copy in f1x:
        copy.start()

    for copy in f1x:
        copy.wait_recv()

    def stage_l1x(b):
        for k in range(2):
            e1[b, k, 72:73, :] = f1x_r[b, k, :, :]
            eb[b, k, :, :] = box_rows(e1, (b, k), 64)

    def deep(b, k):
        return jnp.maximum(jnp.maximum(eb[b, k], eb[b + 1, k]), eb[b + 2, k])

    def stage_o1(b):
        for k in range(2):
            deepest = deep(b, k)
            o1[b + HALF * k, :, :] = deepest[:, :64]
            if k == 0:
                o1[b + BLK, :, :] = roll(deepest, 64, 1)[:, :64]

    def stage_o1_rest(b):
        o1[b + HALF + BLK, :, :] = roll(deep(b, 1), 64, 1)[:, :64]

    def finish_l1():
        half = lane_ids(64) < 64
        for b in range(2):
            later = roll(eb[b, 1], 64, 1)
            eb[BLK + b, 0] = jnp.where(half, roll(eb[b, 0], 64, 1), later)
            eb[BLK + b, 1] = later
        loop(0, BLK, stage_o1)
        loop(0, OUT - HALF - BLK, stage_o1_rest)

    loop(0, BLK, stage_l1x)
    finish_l1()

    def stage_y3(c):
        rows = []
        for g in range(4):
            t3[c, g, 6:8, :] = t3_r[c, g, :, :]
            p3[c, g, 7:8, :] = f3p_r[0, c, g, :, :]
            p3[c, g, 24:25, :] = f3p_r[1, c, g, :, :]
            low, high = split(t3, (c, g), 6, 24)
            high = jnp.abs(high)
            detail = jnp.maximum(high, roll(jnp.maximum(jnp.abs(low), high), 104, 1))
            c3[c, g, :, :] = jnp.maximum(detail, p3[c, g, pl.ds(7, 24), :])
            boxed = jnp.maximum(c3[c, g, pl.ds(0, 16), :], c3[c, g, pl.ds(1, 16), :])
            rows.append(jnp.maximum(boxed, c3[c, g, pl.ds(2, 16), :]))
        x3[c, :, :] = jnp.concatenate(rows + rows, axis=0).T

    for copy in hy3 + f3p:
        copy.wait_recv()
    loop(0, TWO, stage_y3)

    for copy in f2y:
        copy.wait_recv()

    offsets = (0, HALF, BLK, HALF + BLK)

    def spread(block, w, unit, b):
        n = block.shape[0]
        spun = [roll(block, unit * d, 1) if d else block for d in range(4)]
        group = lax.rem(lane_ids(n) // unit, 4)
        for g in range(4):
            full = spun[(3 - g) % 4]
            for r in range(3):
                full = jnp.where(group == r, spun[(r - g) % 4], full)
            w[pl.ds(b + offsets[g], n, stride=PITCH), :] = full

    for c in range(QUAD):
        rows = []
        for g in range(4):
            y2[c, g, 7:8, :] = f2y_r[0, c, g, :, :]
            y2[c, g, 40:41, :] = f2y_r[1, c, g, :, :]
            rows.append(box_rows(y2, (c, g), 32))
        turned = jnp.concatenate(rows, axis=0).T
        for k in range(min(4, BLK - 4 * c)):
            block = turned[32 * k : 32 * k + 32]
            spread(block, w2, 32, 4 * c + k)

    def planes_last(w, out, m, unit):
        count = 128 // unit
        group = lane_ids(40) // unit
        merged = None
        for r in range(count):
            start = pl.multiple_of((m * count + r) * PITCH, 8)
            deepest = w[pl.ds(start, 40), :]
            for shift in (1, 2):
                deepest = jnp.maximum(deepest, w[pl.ds(start + shift, 40), :])
            merged = deepest if r == 0 else jnp.where(group == r, deepest, merged)
        turned = merged.T
        for r in range(count):
            out[m * count + r, :, :] = turned[unit * r : unit * r + unit, :OUT]

    loop(0, 8, lambda m: planes_last(w2, o2, m, 32))

    for c in range(TWO):
        for k in range(2):
            block = x3[c, pl.ds(64 * k, 16), :]
            for shift in (1, 2):
                block = jnp.maximum(block, x3[c, pl.ds(64 * k + shift, 16), :])
            spread(block, w3, 16, 2 * c + k)

    loop(0, 2, lambda m: planes_last(w3, o3, m, 16))

    for row in hx1 + hy1 + [[hs1], hs2, f1y, hx2, fp, f1x, hy3, f3p, f2y]:
        for copy in row:
            copy.wait_send()


def write_out(a1, a2, a3, b1, b2, b3, sems):
    copies = [
        pltpu.make_async_copy(src, dst, sems.at[k])
        for k, (src, dst) in enumerate(((a1, b1), (a2, b2), (a3, b3)))
    ]
    for copy in copies:
        copy.start()
    for copy in copies:
        copy.wait()


def shards(vorticity):
    f32 = jnp.float32
    copies = 5 * len(CHUNKS) + 14
    rows = lambda *shape: pltpu.VMEM(shape, f32)
    pair = lambda *shape: [rows(*shape, 128)] * 2
    results = [
        jax.ShapeDtypeStruct((OUT, 64, 64), f32),
        jax.ShapeDtypeStruct((32, 32, OUT), f32),
        jax.ShapeDtypeStruct((16, 16, OUT), f32),
    ]
    inner = pl.pallas_call(
        kernel,
        out_shape=results,
        in_specs=[pl.BlockSpec(memory_space=pltpu.HBM)],
        out_specs=[pl.BlockSpec(memory_space=pltpu.VMEM)] * 3,
        scratch_shapes=[
            rows(Z, 136, 128),
            rows(Z, 136, 128),
            rows(HALF, 72, 128),
            rows(HALF, 80, 128),
            rows(BLK, 2, 88, 128),
            rows(BLK, 56, 128),
            rows(BLK, 56, 128),
            rows(BLK, 48, 128),
            rows(5, 128, 128),
            rows(TWO, 4, 64, 128),
            rows(TWO, 128, 128),
            rows(TWO, 4, 32, 128),
            rows(TWO, 4, 24, 128),
            rows(BLK, 2, 80, 128),
            rows(BLK + 2, 2, 64, 128),
            rows(QUAD, 4, 48, 128),
            rows(32 * PITCH, 128),
            rows(TWO, 128, 128),
            rows(16 * PITCH, 128),
            *pair(HALF, 8),
            rows(HALF, 16, 128),
            *pair(2, HALF, 1),
            *pair(BLK, 2, 1),
            *pair(BLK, 2),
            rows(Z, 16, 128),
            rows(16 * STRIPS, 8, 128),
            rows(STRIPS, 152, 128),
            rows(STRIPS, 80, 128),
            rows(STRIPS, 80, 128),
            rows(16 * STRIPS, 8, 128),
            rows(16 * STRIPS, 8, 128),
            *pair(2, QUAD, 4, 1),
            *pair(2, TWO, 4, 1),
            *pair(TWO, 4, 2),
            pltpu.SemaphoreType.DMA((2 * len(CHUNKS) + 1,)),
            pltpu.SemaphoreType.DMA((copies,)),
            pltpu.SemaphoreType.DMA((copies,)),
        ],
        compiler_params=pltpu.CompilerParams(
            collective_id=0, has_side_effects=True, vmem_limit_bytes=51 * 2**20
        ),
    )(vorticity)
    o1, o2, o3 = pl.pallas_call(
        write_out,
        out_shape=results,
        in_specs=[pl.BlockSpec(memory_space=pl.ANY)] * 3,
        out_specs=[pl.BlockSpec(memory_space=pl.ANY)] * 3,
        scratch_shapes=[pltpu.SemaphoreType.DMA((3,))],
        compiler_params=pltpu.CompilerParams(vmem_limit_bytes=2**20),
    )(*inner)
    return o1, jnp.transpose(o2, (2, 0, 1)), jnp.transpose(o3, (2, 0, 1))


def solution(mesh):
    placed = P(None, "gx", "gy")
    return jax.shard_map(
        shards, mesh=mesh, in_specs=(placed,), out_specs=(placed,) * 3, check_vma=False
    )
```

```python
import functools

import jax
import jax.numpy as jnp
from jax import lax
from jax.experimental import pallas as pl
from jax.experimental.pallas import tpu as pltpu
from jax.sharding import PartitionSpec as P

H = (
    0.3326705529509569,
    0.8068915093133388,
    0.4598775021193313,
    -0.13501102001039084,
    -0.08544127388224149,
    0.035226291882100656,
)
G = tuple((-1) ** t * H[5 - t] for t in range(6))
Z = 38
HALF = 20
BLK = 10
QUAD = 3
TWO = 5
STRIPS = 3
HR = 4
OUT = Z - 2
PITCH = 48
UNROLL = 5
CHUNKS = ((0, 10), (10, 20))
MESH = pl.DeviceIdType.MESH
roll = pltpu.roll


def lane_ids(rows):
    return lax.broadcasted_iota(jnp.int32, (rows, 128), 1)


def split(ref, lead, start, n):
    low = high = None
    for t in range(6):
        tap = ref[lead + (pl.ds(start + t, n, stride=2), slice(None))]
        low = tap * H[t] if low is None else low + tap * H[t]
        high = tap * G[t] if high is None else high + tap * G[t]
    return low, high


def pool_rows(ref, lead, start, n):
    return jnp.maximum(
        ref[lead + (pl.ds(start, n, stride=2), slice(None))],
        ref[lead + (pl.ds(start + 1, n, stride=2), slice(None))],
    )


def box_rows(ref, lead, n):
    return jnp.maximum(
        jnp.maximum(
            ref[lead + (pl.ds(7, n), slice(None))],
            ref[lead + (pl.ds(9, n), slice(None))],
        ),
        ref[lead + (pl.ds(8, n), slice(None))],
    )


def pair_of(q):
    return jnp.minimum(q + HALF, Z - 1)


def loop(lo, hi, body):
    def step(i, _):
        body(i)
        return 0

    lax.fori_loop(lo, hi, step, 0, unroll=min(UNROLL, hi - lo))


def kernel(
    v, o1, o2, o3,
    vb, tb, s1, d1, t2, s2, c2, pc, p1, t3, p2, p3, c3, e1, eb, y2, w2, x3, w3,
    lk_s, lk_r, lh, f1y_s, f1y_r, f1x_s, f1x_r, fp_s, fp_r, sl, us, ts, ss, ds, ta, tx,
    f2y_s, f2y_r, f3p_s, f3p_r, t3_s, t3_r,
    in_sem, send_sem, recv_sem,
):
    nx, ny = lax.axis_size("gx"), lax.axis_size("gy")
    ix, iy = lax.axis_index("gx"), lax.axis_index("gy")
    x_prev = (lax.rem(ix + nx - 1, nx), iy)
    x_next = (lax.rem(ix + 1, nx), iy)
    y_prev = (ix, lax.rem(iy + ny - 1, ny))
    y_next = (ix, lax.rem(iy + 1, ny))
    counter = [0]

    def remote(src, dst, target):
        k = counter[0]
        counter[0] += 1
        return pltpu.make_async_remote_copy(
            src_ref=src, dst_ref=dst, send_sem=send_sem.at[k], recv_sem=recv_sem.at[k],
            device_id=target, device_id_type=MESH,
        )

    def frames(send, recv, prev, following):
        return [
            remote(send.at[0], recv.at[1], prev),
            remote(send.at[1], recv.at[0], following),
        ]

    spans = []
    for q0, q1 in CHUNKS:
        spans.append(((q0, q1), (q0 + HALF, min(q1 + HALF, Z))))
    loads, hx1, hy1, hk1 = [], [], [], []
    for number, pieces in enumerate(spans):
        row = []
        for part, (a, b) in enumerate(pieces):
            row.append(
                pltpu.make_async_copy(
                    v.at[pl.ds(a, b - a)], vb.at[pl.ds(a, b - a), pl.ds(0, 128)],
                    in_sem.at[2 * number + part],
                )
            )
        loads.append(row)
    for row in loads:
        for copy in row:
            copy.start()
    edge = pltpu.make_async_copy(
        v.at[:, pl.ds(0, 8)], sl.at[:, pl.ds(8, 8)], in_sem.at[2 * len(CHUNKS)]
    )
    edge.start()

    barrier = pltpu.get_barrier_semaphore()
    for device in (x_prev, x_next, y_prev, y_next):
        pl.semaphore_signal(barrier, inc=1, device_id=device, device_id_type=MESH)

    for pieces in spans:
        hx1.append([
            remote(
                v.at[pl.ds(a, b - a), pl.ds(0, HR)],
                vb.at[pl.ds(a, b - a), pl.ds(128, HR)], x_prev,
            )
            for a, b in pieces
        ])
    hs1 = remote(v.at[:, pl.ds(120, 8)], sl.at[:, pl.ds(0, 8)], x_next)
    for (q0, q1), pieces in zip(CHUNKS, spans):
        row = [
            remote(
                tb.at[pl.ds(a, b - a), pl.ds(0, HR)],
                tb.at[pl.ds(a, b - a), pl.ds(128, HR)], y_prev,
            )
            for a, b in pieces
        ]
        hy1.append(row)
        hk1.append(
            remote(lk_s.at[pl.ds(q0, q1 - q0)], lk_r.at[pl.ds(q0, q1 - q0)], y_prev)
        )

    def stage_x1(p):
        lows, highs = [], []
        for piece in range(2):
            low, high = split(vb, (p,), 64 * piece, 32)
            lows.append(low)
            highs.append(high)
        tb[p, pl.ds(0, 128), :] = jnp.concatenate(lows + highs, axis=0).T

    def both(ref, q, start, n):
        later = roll(ref[pair_of(q), pl.ds(start, n), :], 64, 1)
        return jnp.where(lane_ids(n) < 64, ref[q, pl.ds(start, n), :], later)

    def stage_k1(q):
        lk_s[q, :, :] = both(tb, q, HR, 8)

    def begin(number):
        for copy in loads[number]:
            copy.wait()
        for copy in hx1[number]:
            copy.wait_recv()
        for a, b in spans[number]:
            loop(a, b, stage_x1)

    def send(number):
        for copy in hy1[number]:
            copy.start()

    even = lax.rem(ix, 2) == 0

    @pl.when(even)
    def _():
        for number in range(len(CHUNKS)):
            begin(number)
            loop(*CHUNKS[number], stage_k1)

    pl.semaphore_wait(barrier, 4)

    hs1.start()
    for row in hx1:
        for copy in row:
            copy.start()

    @pl.when(even)
    def _():
        for number in range(len(CHUNKS)):
            send(number)
        for copy in hk1:
            copy.start()

    @pl.when(jnp.logical_not(even))
    def _():
        for number in range(len(CHUNKS)):
            begin(number)
            send(number)
            loop(*CHUNKS[number], stage_k1)
            hk1[number].start()

    def stage_xs(p):
        low, high = split(sl, (jnp.minimum(p, Z - 1),), 0, 4)
        us[p, 0:4, :] = low
        us[p, 4:8, :] = high

    def stage_ts(i):
        ts[i, pl.ds(8, 128), :] = us[pl.ds(16 * i, 16)].reshape(128, 128).T

    edge.wait()
    hs1.wait_recv()
    loop(0, 16 * STRIPS, stage_xs)
    loop(0, STRIPS, stage_ts)
    hs2 = [
        remote(ts.at[:, pl.ds(8, 16)], ts.at[:, pl.ds(136, 16)], y_prev),
        remote(ts.at[:, pl.ds(128, 8)], ts.at[:, pl.ds(0, 8)], y_next),
    ]
    for copy in hs2:
        copy.start()

    def stage_ys(i):
        low, high = split(ts, (i,), 6, 70)
        high = jnp.abs(high)
        ss[i, pl.ds(7, 70), :] = low
        ds[i, pl.ds(7, 70), :] = jnp.maximum(
            high, roll(jnp.maximum(jnp.abs(low), high), 124, 1)
        )

    def stage_zs(i):
        low, high = split(ss, (i,), 8, 32)
        pooled = pool_rows(ds, (i,), 8, 32)
        turned = jnp.concatenate([low, high, pooled, pooled], axis=0).T
        ta[pl.ds(16 * i, 16)] = turned.reshape(16, 8, 128)
        boxed = box_rows(ds, (i,), 64)
        turned = jnp.concatenate([boxed, boxed], axis=0).T
        tx[pl.ds(16 * i, 16)] = turned.reshape(16, 8, 128)

    def stage_left(b):
        four, two = lane_ids(4), lane_ids(2)
        pooled = []
        for k in range(2):
            p = b + HALF * k
            t2[b, k, 4:8, :] = jnp.where(
                four < 64, ta[p, 0:4, :], roll(ta[p + BLK, 0:4, :], 64, 1)
            )
            e1[b, k, 7:8, :] = jnp.where(
                lane_ids(1) < 64, tx[p, 3:4, :], tx[p + BLK, 3:4, :]
            )
        for p in (b, b + HALF, b + BLK, b + HALF + BLK):
            pooled.append(pool_rows(ta, (p,), 0, 2))
        lower = roll(jnp.where(two < 96, pooled[0], pooled[1]), 64, 1)
        upper = jnp.where(two < 96, pooled[2], pooled[3])
        pc[b, 6:8, :] = jnp.where(two < 64, lower, upper)

    first = lane_ids(32) < 64

    def stage_y1(q):
        other = pair_of(q)
        for piece in range(2):
            low_a, high_a = split(tb, (q,), 64 * piece, 32)
            low_b, high_b = split(tb, (other,), 64 * piece, 32)
            turned_a, turned_b = roll(low_a, 64, 1), roll(low_b, 64, 1)
            s1[q, pl.ds(32 * piece, 32), :] = jnp.where(first, low_a, turned_b)
            cross = jnp.abs(jnp.where(first, turned_a, low_b))
            high_a, high_b = jnp.abs(high_a), jnp.abs(high_b)
            high_a = jnp.maximum(high_a, roll(high_a, 64, 1))
            high_b = jnp.maximum(high_b, roll(high_b, 64, 1))
            detail = jnp.maximum(jnp.where(first, high_a, high_b), cross)
            d1[q, pl.ds(8 + 32 * piece, 32), :] = detail
            if piece == 0:
                f1y_s[0, q, :, :] = detail[0:1]
            else:
                f1y_s[1, q, :, :] = detail[31:32]

    def stage_k2(q):
        lh[q, pl.ds(0, HR), :] = both(tb, q, 128, HR)
        lh[q, pl.ds(HR, 8), :] = lk_r[q, :, :]
        low = None
        for t in range(6):
            tap = lh[q, pl.ds(t, HR, stride=2), :] * H[t]
            low = tap if low is None else low + tap
        s1[q, pl.ds(64, HR), :] = low

    for number, (q0, q1) in enumerate(CHUNKS):
        for copy in hy1[number]:
            copy.wait_recv()
        loop(q0, q1, stage_y1)
    f1y = frames(f1y_s, f1y_r, y_prev, y_next)
    for copy in f1y:
        copy.start()
    for copy in hk1:
        copy.wait_recv()
    loop(0, HALF, stage_k2)

    quarter = lax.rem(lane_ids(32), 64) < 32

    def stage_p1(b):
        rows = [pool_rows(d1, (b + 5 * k,), 8, 32) for k in range(4)]
        p1[b, :, :] = jnp.concatenate(rows, axis=0).T
        pool_a = pool_rows(p1, (b,), 0, 32)
        pool_b = pool_rows(p1, (b,), 64, 32)
        for block, pooled in (
            (b, jnp.where(quarter, pool_a, roll(pool_b, 32, 1))),
            (b + 5, jnp.where(quarter, roll(pool_a, 96, 1), pool_b)),
        ):
            pc[block, pl.ds(8, 32), :] = pooled
            fp_s[block, :, :] = pooled[0:2]

    def stage_y2(b):
        rows = []
        for q in (b, b + BLK):
            rows += split(s1, (q,), 0, 32)
        turned = jnp.concatenate(rows, axis=0).T
        t2[b, 0, pl.ds(8, 64), :] = turned[:64]
        t2[b, 1, pl.ds(8, 64), :] = turned[64:]

    loop(0, BLK, stage_y2)
    hx2 = [remote(t2.at[:, :, pl.ds(8, 16)], t2.at[:, :, pl.ds(72, 16)], x_prev)]
    for copy in hx2:
        copy.start()
    loop(0, 5, stage_p1)
    fp = [remote(fp_s, fp_r, x_prev)]
    for copy in fp:
        copy.start()

    for copy in hs2:
        copy.wait_recv()
    loop(0, STRIPS, stage_ys)
    loop(0, STRIPS, stage_zs)
    loop(0, BLK, stage_left)

    wide = lax.rem(lane_ids(40), 64) < 32

    def stage_x2(b):
        pc[b, 40:42, :] = fp_r[b, :, :]
        lows, details = [], []
        for k in range(2):
            low, high = split(t2, (b, k), 4, 40)
            high = jnp.abs(high)
            lows.append(low)
            details.append(
                jnp.maximum(high, roll(jnp.maximum(jnp.abs(low), high), 96, 1))
            )
        s2[b, pl.ds(0, 40), :] = jnp.where(wide, lows[0], roll(lows[1], 32, 1))
        detail = jnp.where(wide, details[0], roll(details[1], 32, 1))
        c2[b, pl.ds(6, 40), :] = jnp.maximum(detail, pc[b, pl.ds(6, 40), :])

    for copy in hx2 + fp:
        copy.wait_recv()
    loop(0, BLK, stage_x2)

    def stage_l2x(c):
        rows = [box_rows(c2, (jnp.minimum(4 * c + k, BLK - 1),), 32) for k in range(4)]
        turned = jnp.concatenate(rows, axis=0).T
        for g in range(4):
            y2[c, g, pl.ds(8, 32), :] = turned[32 * g : 32 * g + 32]
            f2y_s[0, c, g, :, :] = turned[32 * g : 32 * g + 1]
            f2y_s[1, c, g, :, :] = turned[32 * g + 31 : 32 * g + 32]

    loop(0, QUAD, stage_l2x)
    f2y = frames(f2y_s, f2y_r, y_prev, y_next)
    for copy in f2y:
        copy.start()

    def stage_x3(c):
        rows = []
        for k in range(2):
            low, high = split(s2, (2 * c + k,), 0, 24)
            rows += [low, high, low[:16]]
        turned = jnp.concatenate(rows, axis=0).T
        for g in range(4):
            piece = turned[32 * g : 32 * g + 32]
            t3[c, g, pl.ds(8, 32), :] = piece
            t3_s[c, g, :, :] = piece[30:32]

    loop(0, TWO, stage_x3)
    hy3 = [
        remote(t3.at[:, :, pl.ds(8, 6)], t3.at[:, :, pl.ds(40, 6)], y_prev),
        remote(t3_s, t3_r, y_next),
    ]
    for copy in hy3:
        copy.start()

    def stage_p2(c):
        rows = []
        for k in range(2):
            pooled = pool_rows(c2, (2 * c + k,), 6, 24)
            rows += [pooled, pooled, pooled[:16]]
        p2[c, :, :] = jnp.concatenate(rows, axis=0).T
        for g in range(4):
            pooled = pool_rows(p2, (c,), 32 * g, 16)
            p3[c, g, pl.ds(8, 16), :] = pooled
            f3p_s[0, c, g, :, :] = pooled[0:1]
            f3p_s[1, c, g, :, :] = pooled[15:16]

    loop(0, TWO, stage_p2)
    f3p = frames(f3p_s, f3p_r, y_prev, y_next)
    for copy in f3p:
        copy.start()

    for copy in f1y:
        copy.wait_recv()

    def stage_l1y(b):
        rows = []
        for q in (b, b + BLK):
            d1[q, 7:8, :] = f1y_r[0, q, :, :]
            d1[q, 72:73, :] = f1y_r[1, q, :, :]
            rows.append(box_rows(d1, (q,), 64))
        turned = jnp.concatenate(rows, axis=0).T
        for k in range(2):
            e1[b, k, pl.ds(8, 64), :] = turned[64 * k : 64 * k + 64]
            f1x_s[b, k, :, :] = turned[64 * k : 64 * k + 1]

    loop(0, BLK, stage_l1y)
    f1x = [remote(f1x_s, f1x_r, x_prev)]
    for copy in f1x:
        copy.start()

    for copy in f2y:
        copy.wait_recv()

    offsets = (0, HALF, BLK, HALF + BLK)

    def spread(block, w, unit, b):
        n = block.shape[0]
        spun = [roll(block, unit * d, 1) if d else block for d in range(4)]
        group = lax.rem(lane_ids(n) // unit, 4)
        for g in range(4):
            full = spun[(3 - g) % 4]
            for r in range(3):
                full = jnp.where(group == r, spun[(r - g) % 4], full)
            w[pl.ds(b + offsets[g], n, stride=PITCH), :] = full

    for c in range(QUAD):
        rows = []
        for g in range(4):
            y2[c, g, 7:8, :] = f2y_r[0, c, g, :, :]
            y2[c, g, 40:41, :] = f2y_r[1, c, g, :, :]
            rows.append(box_rows(y2, (c, g), 32))
        turned = jnp.concatenate(rows, axis=0).T
        for k in range(min(4, BLK - 4 * c)):
            block = turned[32 * k : 32 * k + 32]
            spread(block, w2, 32, 4 * c + k)

    def planes_last(w, out, m, unit):
        count = 128 // unit
        group = lane_ids(40) // unit
        merged = None
        for r in range(count):
            start = pl.multiple_of((m * count + r) * PITCH, 8)
            deepest = w[pl.ds(start, 40), :]
            for shift in (1, 2):
                deepest = jnp.maximum(deepest, w[pl.ds(start + shift, 40), :])
            merged = deepest if r == 0 else jnp.where(group == r, deepest, merged)
        turned = merged.T
        for r in range(count):
            out[m * count + r, :, :] = turned[unit * r : unit * r + unit, :OUT]

    loop(0, 8, lambda m: planes_last(w2, o2, m, 32))

    for copy in f1x:
        copy.wait_recv()

    def stage_l1x(b):
        for k in range(2):
            e1[b, k, 72:73, :] = f1x_r[b, k, :, :]
            eb[b, k, :, :] = box_rows(e1, (b, k), 64)

    def deep(b, k):
        return jnp.maximum(jnp.maximum(eb[b, k], eb[b + 1, k]), eb[b + 2, k])

    def stage_o1(b):
        for k in range(2):
            deepest = deep(b, k)
            o1[b + HALF * k, :, :] = deepest[:, :64]
            if k == 0:
                o1[b + BLK, :, :] = roll(deepest, 64, 1)[:, :64]

    def stage_o1_rest(b):
        o1[b + HALF + BLK, :, :] = roll(deep(b, 1), 64, 1)[:, :64]

    def finish_l1():
        half = lane_ids(64) < 64
        for b in range(2):
            later = roll(eb[b, 1], 64, 1)
            eb[BLK + b, 0] = jnp.where(half, roll(eb[b, 0], 64, 1), later)
            eb[BLK + b, 1] = later
        loop(0, BLK, stage_o1)
        loop(0, OUT - HALF - BLK, stage_o1_rest)

    loop(0, BLK, stage_l1x)
    finish_l1()

    def stage_y3(c):
        rows = []
        for g in range(4):
            t3[c, g, 6:8, :] = t3_r[c, g, :, :]
            p3[c, g, 7:8, :] = f3p_r[0, c, g, :, :]
            p3[c, g, 24:25, :] = f3p_r[1, c, g, :, :]
            low, high = split(t3, (c, g), 6, 24)
            high = jnp.abs(high)
            detail = jnp.maximum(high, roll(jnp.maximum(jnp.abs(low), high), 104, 1))
            c3[c, g, :, :] = jnp.maximum(detail, p3[c, g, pl.ds(7, 24), :])
            boxed = jnp.maximum(c3[c, g, pl.ds(0, 16), :], c3[c, g, pl.ds(1, 16), :])
            rows.append(jnp.maximum(boxed, c3[c, g, pl.ds(2, 16), :]))
        x3[c, :, :] = jnp.concatenate(rows + rows, axis=0).T

    for copy in hy3 + f3p:
        copy.wait_recv()
    loop(0, TWO, stage_y3)

    for c in range(TWO):
        for k in range(2):
            block = x3[c, pl.ds(64 * k, 16), :]
            for shift in (1, 2):
                block = jnp.maximum(block, x3[c, pl.ds(64 * k + shift, 16), :])
            spread(block, w3, 16, 2 * c + k)

    loop(0, 2, lambda m: planes_last(w3, o3, m, 16))

    for row in hx1 + hy1 + [hk1, [hs1], hs2, f1y, hx2, fp, f1x, hy3, f3p, f2y]:
        for copy in row:
            copy.wait_send()


def write_out(a1, a2, a3, b1, b2, b3, sems):
    copies = [
        pltpu.make_async_copy(src, dst, sems.at[k])
        for k, (src, dst) in enumerate(((a1, b1), (a2, b2), (a3, b3)))
    ]
    for copy in copies:
        copy.start()
    for copy in copies:
        copy.wait()


def shards(vorticity):
    f32 = jnp.float32
    copies = 5 * len(CHUNKS) + 14
    rows = lambda *shape: pltpu.VMEM(shape, f32)
    pair = lambda *shape: [rows(*shape, 128)] * 2
    results = [
        jax.ShapeDtypeStruct((OUT, 64, 64), f32),
        jax.ShapeDtypeStruct((32, 32, OUT), f32),
        jax.ShapeDtypeStruct((16, 16, OUT), f32),
    ]
    inner = pl.pallas_call(
        kernel,
        out_shape=results,
        in_specs=[pl.BlockSpec(memory_space=pltpu.HBM)],
        out_specs=[pl.BlockSpec(memory_space=pltpu.VMEM)] * 3,
        scratch_shapes=[
            rows(Z, 136, 128),
            rows(Z, 136, 128),
            rows(HALF, 72, 128),
            rows(HALF, 80, 128),
            rows(BLK, 2, 88, 128),
            rows(BLK, 56, 128),
            rows(BLK, 56, 128),
            rows(BLK, 48, 128),
            rows(5, 128, 128),
            rows(TWO, 4, 64, 128),
            rows(TWO, 128, 128),
            rows(TWO, 4, 32, 128),
            rows(TWO, 4, 24, 128),
            rows(BLK, 2, 80, 128),
            rows(BLK + 2, 2, 64, 128),
            rows(QUAD, 4, 48, 128),
            rows(32 * PITCH, 128),
            rows(TWO, 128, 128),
            rows(16 * PITCH, 128),
            *pair(HALF, 8),
            rows(HALF, 16, 128),
            *pair(2, HALF, 1),
            *pair(BLK, 2, 1),
            *pair(BLK, 2),
            rows(Z, 16, 128),
            rows(16 * STRIPS, 8, 128),
            rows(STRIPS, 152, 128),
            rows(STRIPS, 80, 128),
            rows(STRIPS, 80, 128),
            rows(16 * STRIPS, 8, 128),
            rows(16 * STRIPS, 8, 128),
            *pair(2, QUAD, 4, 1),
            *pair(2, TWO, 4, 1),
            *pair(TWO, 4, 2),
            pltpu.SemaphoreType.DMA((2 * len(CHUNKS) + 1,)),
            pltpu.SemaphoreType.DMA((copies,)),
            pltpu.SemaphoreType.DMA((copies,)),
        ],
        compiler_params=pltpu.CompilerParams(
            collective_id=0, has_side_effects=True, vmem_limit_bytes=51 * 2**20
        ),
    )(vorticity)
    o1, o2, o3 = pl.pallas_call(
        write_out,
        out_shape=results,
        in_specs=[pl.BlockSpec(memory_space=pl.ANY)] * 3,
        out_specs=[pl.BlockSpec(memory_space=pl.ANY)] * 3,
        scratch_shapes=[pltpu.SemaphoreType.DMA((3,))],
        compiler_params=pltpu.CompilerParams(vmem_limit_bytes=2**20),
    )(*inner)
    return o1, jnp.transpose(o2, (2, 0, 1)), jnp.transpose(o3, (2, 0, 1))


def solution(mesh):
    placed = P(None, "gx", "gy")
    return jax.shard_map(
        shards, mesh=mesh, in_specs=(placed,), out_specs=(placed,) * 3, check_vma=False
    )
```

```python
import functools

import jax
import jax.numpy as jnp
from jax import lax
from jax.experimental import pallas as pl
from jax.experimental.pallas import tpu as pltpu
from jax.sharding import PartitionSpec as P

H = (
    0.3326705529509569,
    0.8068915093133388,
    0.4598775021193313,
    -0.13501102001039084,
    -0.08544127388224149,
    0.035226291882100656,
)
G = tuple((-1) ** t * H[5 - t] for t in range(6))
Z = 38
HALF = 20
BLK = 10
QUAD = 3
TWO = 5
STRIPS = 3
HR = 4
OUT = Z - 2
PITCH = 48
UNROLL = 10
CHUNKS = ((0, 10), (10, 20))
MESH = pl.DeviceIdType.MESH
roll = pltpu.roll


def lane_ids(rows):
    return lax.broadcasted_iota(jnp.int32, (rows, 128), 1)


def split(ref, lead, start, n):
    low = high = None
    for t in range(6):
        tap = ref[lead + (pl.ds(start + t, n, stride=2), slice(None))]
        low = tap * H[t] if low is None else low + tap * H[t]
        high = tap * G[t] if high is None else high + tap * G[t]
    return low, high


def pool_rows(ref, lead, start, n):
    return jnp.maximum(
        ref[lead + (pl.ds(start, n, stride=2), slice(None))],
        ref[lead + (pl.ds(start + 1, n, stride=2), slice(None))],
    )


def box_rows(ref, lead, n):
    return jnp.maximum(
        jnp.maximum(
            ref[lead + (pl.ds(7, n), slice(None))],
            ref[lead + (pl.ds(9, n), slice(None))],
        ),
        ref[lead + (pl.ds(8, n), slice(None))],
    )


def pair_of(q):
    return jnp.minimum(q + HALF, Z - 1)


def loop(lo, hi, body):
    def step(i, _):
        body(i)
        return 0

    lax.fori_loop(lo, hi, step, 0, unroll=min(UNROLL, hi - lo))


def kernel(
    v, o1, o2, o3,
    vb, tb, s1, d1, t2, s2, c2, pc, p1, t3, p2, p3, c3, e1, eb, y2, w2, x3, w3,
    lk_s, lk_r, lh, f1y_s, f1y_r, f1x_s, f1x_r, fp_s, fp_r, sl, us, ts, ss, ds, ta, tx,
    f2y_s, f2y_r, f3p_s, f3p_r, t3_s, t3_r,
    in_sem, send_sem, recv_sem,
):
    nx, ny = lax.axis_size("gx"), lax.axis_size("gy")
    ix, iy = lax.axis_index("gx"), lax.axis_index("gy")
    x_prev = (lax.rem(ix + nx - 1, nx), iy)
    x_next = (lax.rem(ix + 1, nx), iy)
    y_prev = (ix, lax.rem(iy + ny - 1, ny))
    y_next = (ix, lax.rem(iy + 1, ny))
    counter = [0]

    def remote(src, dst, target):
        k = counter[0]
        counter[0] += 1
        return pltpu.make_async_remote_copy(
            src_ref=src, dst_ref=dst, send_sem=send_sem.at[k], recv_sem=recv_sem.at[k],
            device_id=target, device_id_type=MESH,
        )

    def frames(send, recv, prev, following):
        return [
            remote(send.at[0], recv.at[1], prev),
            remote(send.at[1], recv.at[0], following),
        ]

    spans = []
    for q0, q1 in CHUNKS:
        spans.append(((q0, q1), (q0 + HALF, min(q1 + HALF, Z))))
    loads, hx1, hy1, hk1 = [], [], [], []
    for number, pieces in enumerate(spans):
        row = []
        for part, (a, b) in enumerate(pieces):
            row.append(
                pltpu.make_async_copy(
                    v.at[pl.ds(a, b - a)], vb.at[pl.ds(a, b - a), pl.ds(0, 128)],
                    in_sem.at[2 * number + part],
                )
            )
        loads.append(row)
    for row in loads:
        for copy in row:
            copy.start()
    edge = pltpu.make_async_copy(
        v.at[:, pl.ds(0, 8)], sl.at[:, pl.ds(8, 8)], in_sem.at[2 * len(CHUNKS)]
    )
    edge.start()

    barrier = pltpu.get_barrier_semaphore()
    for device in (x_prev, x_next, y_prev, y_next):
        pl.semaphore_signal(barrier, inc=1, device_id=device, device_id_type=MESH)

    for pieces in spans:
        hx1.append([
            remote(
                v.at[pl.ds(a, b - a), pl.ds(0, HR)],
                vb.at[pl.ds(a, b - a), pl.ds(128, HR)], x_prev,
            )
            for a, b in pieces
        ])
    hs1 = remote(v.at[:, pl.ds(120, 8)], sl.at[:, pl.ds(0, 8)], x_next)
    for (q0, q1), pieces in zip(CHUNKS, spans):
        row = [
            remote(
                tb.at[pl.ds(a, b - a), pl.ds(0, HR)],
                tb.at[pl.ds(a, b - a), pl.ds(128, HR)], y_prev,
            )
            for a, b in pieces
        ]
        hy1.append(row)
        hk1.append(
            remote(lk_s.at[pl.ds(q0, q1 - q0)], lk_r.at[pl.ds(q0, q1 - q0)], y_prev)
        )

    def stage_x1(p):
        lows, highs = [], []
        for piece in range(2):
            low, high = split(vb, (p,), 64 * piece, 32)
            lows.append(low)
            highs.append(high)
        tb[p, pl.ds(0, 128), :] = jnp.concatenate(lows + highs, axis=0).T

    def both(ref, q, start, n):
        later = roll(ref[pair_of(q), pl.ds(start, n), :], 64, 1)
        return jnp.where(lane_ids(n) < 64, ref[q, pl.ds(start, n), :], later)

    def stage_k1(q):
        lk_s[q, :, :] = both(tb, q, HR, 8)

    def begin(number):
        for copy in loads[number]:
            copy.wait()
        for copy in hx1[number]:
            copy.wait_recv()
        for a, b in spans[number]:
            loop(a, b, stage_x1)

    def send(number):
        for copy in hy1[number]:
            copy.start()

    even = lax.rem(ix, 2) == 0

    @pl.when(even)
    def _():
        for number in range(len(CHUNKS)):
            begin(number)
            loop(*CHUNKS[number], stage_k1)

    pl.semaphore_wait(barrier, 4)

    hs1.start()
    for row in hx1:
        for copy in row:
            copy.start()

    @pl.when(even)
    def _():
        for number in range(len(CHUNKS)):
            send(number)
        for copy in hk1:
            copy.start()

    @pl.when(jnp.logical_not(even))
    def _():
        for number in range(len(CHUNKS)):
            begin(number)
            send(number)
            loop(*CHUNKS[number], stage_k1)
            hk1[number].start()

    def stage_xs(p):
        low, high = split(sl, (jnp.minimum(p, Z - 1),), 0, 4)
        us[p, 0:4, :] = low
        us[p, 4:8, :] = high

    def stage_ts(i):
        ts[i, pl.ds(8, 128), :] = us[pl.ds(16 * i, 16)].reshape(128, 128).T

    edge.wait()
    hs1.wait_recv()
    loop(0, 16 * STRIPS, stage_xs)
    loop(0, STRIPS, stage_ts)
    hs2 = [
        remote(ts.at[:, pl.ds(8, 16)], ts.at[:, pl.ds(136, 16)], y_prev),
        remote(ts.at[:, pl.ds(128, 8)], ts.at[:, pl.ds(0, 8)], y_next),
    ]
    for copy in hs2:
        copy.start()

    def stage_ys(i):
        low, high = split(ts, (i,), 6, 70)
        high = jnp.abs(high)
        ss[i, pl.ds(7, 70), :] = low
        ds[i, pl.ds(7, 70), :] = jnp.maximum(
            high, roll(jnp.maximum(jnp.abs(low), high), 124, 1)
        )

    def stage_zs(i):
        low, high = split(ss, (i,), 8, 32)
        pooled = pool_rows(ds, (i,), 8, 32)
        turned = jnp.concatenate([low, high, pooled, pooled], axis=0).T
        ta[pl.ds(16 * i, 16)] = turned.reshape(16, 8, 128)
        boxed = box_rows(ds, (i,), 64)
        turned = jnp.concatenate([boxed, boxed], axis=0).T
        tx[pl.ds(16 * i, 16)] = turned.reshape(16, 8, 128)

    def stage_left(b):
        four, two = lane_ids(4), lane_ids(2)
        pooled = []
        for k in range(2):
            p = b + HALF * k
            t2[b, k, 4:8, :] = jnp.where(
                four < 64, ta[p, 0:4, :], roll(ta[p + BLK, 0:4, :], 64, 1)
            )
            e1[b, k, 7:8, :] = jnp.where(
                lane_ids(1) < 64, tx[p, 3:4, :], tx[p + BLK, 3:4, :]
            )
        for p in (b, b + HALF, b + BLK, b + HALF + BLK):
            pooled.append(pool_rows(ta, (p,), 0, 2))
        lower = roll(jnp.where(two < 96, pooled[0], pooled[1]), 64, 1)
        upper = jnp.where(two < 96, pooled[2], pooled[3])
        pc[b, 6:8, :] = jnp.where(two < 64, lower, upper)

    first = lane_ids(32) < 64

    def stage_y1(q):
        other = pair_of(q)
        for piece in range(2):
            low_a, high_a = split(tb, (q,), 64 * piece, 32)
            low_b, high_b = split(tb, (other,), 64 * piece, 32)
            turned_a, turned_b = roll(low_a, 64, 1), roll(low_b, 64, 1)
            s1[q, pl.ds(32 * piece, 32), :] = jnp.where(first, low_a, turned_b)
            cross = jnp.abs(jnp.where(first, turned_a, low_b))
            high_a, high_b = jnp.abs(high_a), jnp.abs(high_b)
            high_a = jnp.maximum(high_a, roll(high_a, 64, 1))
            high_b = jnp.maximum(high_b, roll(high_b, 64, 1))
            detail = jnp.maximum(jnp.where(first, high_a, high_b), cross)
            d1[q, pl.ds(8 + 32 * piece, 32), :] = detail
            if piece == 0:
                f1y_s[0, q, :, :] = detail[0:1]
            else:
                f1y_s[1, q, :, :] = detail[31:32]

    def stage_k2(q):
        lh[q, pl.ds(0, HR), :] = both(tb, q, 128, HR)
        lh[q, pl.ds(HR, 8), :] = lk_r[q, :, :]
        low = None
        for t in range(6):
            tap = lh[q, pl.ds(t, HR, stride=2), :] * H[t]
            low = tap if low is None else low + tap
        s1[q, pl.ds(64, HR), :] = low

    for number, (q0, q1) in enumerate(CHUNKS):
        for copy in hy1[number]:
            copy.wait_recv()
        loop(q0, q1, stage_y1)
    f1y = frames(f1y_s, f1y_r, y_prev, y_next)
    for copy in f1y:
        copy.start()
    for copy in hk1:
        copy.wait_recv()
    loop(0, HALF, stage_k2)

    quarter = lax.rem(lane_ids(32), 64) < 32

    def stage_p1(b):
        rows = [pool_rows(d1, (b + 5 * k,), 8, 32) for k in range(4)]
        p1[b, :, :] = jnp.concatenate(rows, axis=0).T
        pool_a = pool_rows(p1, (b,), 0, 32)
        pool_b = pool_rows(p1, (b,), 64, 32)
        for block, pooled in (
            (b, jnp.where(quarter, pool_a, roll(pool_b, 32, 1))),
            (b + 5, jnp.where(quarter, roll(pool_a, 96, 1), pool_b)),
        ):
            pc[block, pl.ds(8, 32), :] = pooled
            fp_s[block, :, :] = pooled[0:2]

    def stage_y2(b):
        rows = []
        for q in (b, b + BLK):
            rows += split(s1, (q,), 0, 32)
        turned = jnp.concatenate(rows, axis=0).T
        t2[b, 0, pl.ds(8, 64), :] = turned[:64]
        t2[b, 1, pl.ds(8, 64), :] = turned[64:]

    loop(0, BLK, stage_y2)
    hx2 = [remote(t2.at[:, :, pl.ds(8, 16)], t2.at[:, :, pl.ds(72, 16)], x_prev)]
    for copy in hx2:
        copy.start()
    loop(0, 5, stage_p1)
    fp = [remote(fp_s, fp_r, x_prev)]
    for copy in fp:
        copy.start()

    for copy in hs2:
        copy.wait_recv()
    loop(0, STRIPS, stage_ys)
    loop(0, STRIPS, stage_zs)
    loop(0, BLK, stage_left)

    wide = lax.rem(lane_ids(40), 64) < 32

    def stage_x2(b):
        pc[b, 40:42, :] = fp_r[b, :, :]
        lows, details = [], []
        for k in range(2):
            low, high = split(t2, (b, k), 4, 40)
            high = jnp.abs(high)
            lows.append(low)
            details.append(
                jnp.maximum(high, roll(jnp.maximum(jnp.abs(low), high), 96, 1))
            )
        s2[b, pl.ds(0, 40), :] = jnp.where(wide, lows[0], roll(lows[1], 32, 1))
        detail = jnp.where(wide, details[0], roll(details[1], 32, 1))
        c2[b, pl.ds(6, 40), :] = jnp.maximum(detail, pc[b, pl.ds(6, 40), :])

    for copy in hx2 + fp:
        copy.wait_recv()
    loop(0, BLK, stage_x2)

    def stage_l2x(c):
        rows = [box_rows(c2, (jnp.minimum(4 * c + k, BLK - 1),), 32) for k in range(4)]
        turned = jnp.concatenate(rows, axis=0).T
        for g in range(4):
            y2[c, g, pl.ds(8, 32), :] = turned[32 * g : 32 * g + 32]
            f2y_s[0, c, g, :, :] = turned[32 * g : 32 * g + 1]
            f2y_s[1, c, g, :, :] = turned[32 * g + 31 : 32 * g + 32]

    loop(0, QUAD, stage_l2x)
    f2y = frames(f2y_s, f2y_r, y_prev, y_next)
    for copy in f2y:
        copy.start()

    def stage_x3(c):
        rows = []
        for k in range(2):
            low, high = split(s2, (2 * c + k,), 0, 24)
            rows += [low, high, low[:16]]
        turned = jnp.concatenate(rows, axis=0).T
        for g in range(4):
            piece = turned[32 * g : 32 * g + 32]
            t3[c, g, pl.ds(8, 32), :] = piece
            t3_s[c, g, :, :] = piece[30:32]

    loop(0, TWO, stage_x3)
    hy3 = [
        remote(t3.at[:, :, pl.ds(8, 6)], t3.at[:, :, pl.ds(40, 6)], y_prev),
        remote(t3_s, t3_r, y_next),
    ]
    for copy in hy3:
        copy.start()

    def stage_p2(c):
        rows = []
        for k in range(2):
            pooled = pool_rows(c2, (2 * c + k,), 6, 24)
            rows += [pooled, pooled, pooled[:16]]
        p2[c, :, :] = jnp.concatenate(rows, axis=0).T
        for g in range(4):
            pooled = pool_rows(p2, (c,), 32 * g, 16)
            p3[c, g, pl.ds(8, 16), :] = pooled
            f3p_s[0, c, g, :, :] = pooled[0:1]
            f3p_s[1, c, g, :, :] = pooled[15:16]

    loop(0, TWO, stage_p2)
    f3p = frames(f3p_s, f3p_r, y_prev, y_next)
    for copy in f3p:
        copy.start()

    for copy in f1y:
        copy.wait_recv()

    def stage_l1y(b):
        rows = []
        for q in (b, b + BLK):
            d1[q, 7:8, :] = f1y_r[0, q, :, :]
            d1[q, 72:73, :] = f1y_r[1, q, :, :]
            rows.append(box_rows(d1, (q,), 64))
        turned = jnp.concatenate(rows, axis=0).T
        for k in range(2):
            e1[b, k, pl.ds(8, 64), :] = turned[64 * k : 64 * k + 64]
            f1x_s[b, k, :, :] = turned[64 * k : 64 * k + 1]

    loop(0, BLK, stage_l1y)
    f1x = [remote(f1x_s, f1x_r, x_prev)]
    for copy in f1x:
        copy.start()

    for copy in f2y:
        copy.wait_recv()

    offsets = (0, HALF, BLK, HALF + BLK)

    def spread(block, w, unit, b):
        n = block.shape[0]
        spun = [roll(block, unit * d, 1) if d else block for d in range(4)]
        group = lax.rem(lane_ids(n) // unit, 4)
        for g in range(4):
            full = spun[(3 - g) % 4]
            for r in range(3):
                full = jnp.where(group == r, spun[(r - g) % 4], full)
            w[pl.ds(b + offsets[g], n, stride=PITCH), :] = full

    for c in range(QUAD):
        rows = []
        for g in range(4):
            y2[c, g, 7:8, :] = f2y_r[0, c, g, :, :]
            y2[c, g, 40:41, :] = f2y_r[1, c, g, :, :]
            rows.append(box_rows(y2, (c, g), 32))
        turned = jnp.concatenate(rows, axis=0).T
        for k in range(min(4, BLK - 4 * c)):
            block = turned[32 * k : 32 * k + 32]
            spread(block, w2, 32, 4 * c + k)

    def planes_last(w, out, m, unit):
        count = 128 // unit
        group = lane_ids(40) // unit
        merged = None
        for r in range(count):
            start = pl.multiple_of((m * count + r) * PITCH, 8)
            deepest = w[pl.ds(start, 40), :]
            for shift in (1, 2):
                deepest = jnp.maximum(deepest, w[pl.ds(start + shift, 40), :])
            merged = deepest if r == 0 else jnp.where(group == r, deepest, merged)
        turned = merged.T
        for r in range(count):
            out[m * count + r, :, :] = turned[unit * r : unit * r + unit, :OUT]

    loop(0, 8, lambda m: planes_last(w2, o2, m, 32))

    for copy in f1x:
        copy.wait_recv()

    def stage_l1x(b):
        for k in range(2):
            e1[b, k, 72:73, :] = f1x_r[b, k, :, :]
            eb[b, k, :, :] = box_rows(e1, (b, k), 64)

    def deep(b, k):
        return jnp.maximum(jnp.maximum(eb[b, k], eb[b + 1, k]), eb[b + 2, k])

    def stage_o1(b):
        for k in range(2):
            deepest = deep(b, k)
            o1[b + HALF * k, :, :] = deepest[:, :64]
            if k == 0:
                o1[b + BLK, :, :] = roll(deepest, 64, 1)[:, :64]

    def stage_o1_rest(b):
        o1[b + HALF + BLK, :, :] = roll(deep(b, 1), 64, 1)[:, :64]

    def finish_l1():
        half = lane_ids(64) < 64
        for b in range(2):
            later = roll(eb[b, 1], 64, 1)
            eb[BLK + b, 0] = jnp.where(half, roll(eb[b, 0], 64, 1), later)
            eb[BLK + b, 1] = later
        loop(0, BLK, stage_o1)
        loop(0, OUT - HALF - BLK, stage_o1_rest)

    loop(0, BLK, stage_l1x)
    finish_l1()

    def stage_y3(c):
        rows = []
        for g in range(4):
            t3[c, g, 6:8, :] = t3_r[c, g, :, :]
            p3[c, g, 7:8, :] = f3p_r[0, c, g, :, :]
            p3[c, g, 24:25, :] = f3p_r[1, c, g, :, :]
            low, high = split(t3, (c, g), 6, 24)
            high = jnp.abs(high)
            detail = jnp.maximum(high, roll(jnp.maximum(jnp.abs(low), high), 104, 1))
            c3[c, g, :, :] = jnp.maximum(detail, p3[c, g, pl.ds(7, 24), :])
            boxed = jnp.maximum(c3[c, g, pl.ds(0, 16), :], c3[c, g, pl.ds(1, 16), :])
            rows.append(jnp.maximum(boxed, c3[c, g, pl.ds(2, 16), :]))
        x3[c, :, :] = jnp.concatenate(rows + rows, axis=0).T

    for copy in hy3 + f3p:
        copy.wait_recv()
    loop(0, TWO, stage_y3)

    for c in range(TWO):
        for k in range(2):
            block = x3[c, pl.ds(64 * k, 16), :]
            for shift in (1, 2):
                block = jnp.maximum(block, x3[c, pl.ds(64 * k + shift, 16), :])
            spread(block, w3, 16, 2 * c + k)

    loop(0, 2, lambda m: planes_last(w3, o3, m, 16))

    for row in hx1 + hy1 + [hk1, [hs1], hs2, f1y, hx2, fp, f1x, hy3, f3p, f2y]:
        for copy in row:
            copy.wait_send()


def write_out(a1, a2, a3, b1, b2, b3, sems):
    copies = [
        pltpu.make_async_copy(src, dst, sems.at[k])
        for k, (src, dst) in enumerate(((a1, b1), (a2, b2), (a3, b3)))
    ]
    for copy in copies:
        copy.start()
    for copy in copies:
        copy.wait()


def shards(vorticity):
    f32 = jnp.float32
    copies = 5 * len(CHUNKS) + 14
    rows = lambda *shape: pltpu.VMEM(shape, f32)
    pair = lambda *shape: [rows(*shape, 128)] * 2
    results = [
        jax.ShapeDtypeStruct((OUT, 64, 64), f32),
        jax.ShapeDtypeStruct((32, 32, OUT), f32),
        jax.ShapeDtypeStruct((16, 16, OUT), f32),
    ]
    inner = pl.pallas_call(
        kernel,
        out_shape=results,
        in_specs=[pl.BlockSpec(memory_space=pltpu.HBM)],
        out_specs=[pl.BlockSpec(memory_space=pltpu.VMEM)] * 3,
        scratch_shapes=[
            rows(Z, 136, 128),
            rows(Z, 136, 128),
            rows(HALF, 72, 128),
            rows(HALF, 80, 128),
            rows(BLK, 2, 88, 128),
            rows(BLK, 56, 128),
            rows(BLK, 56, 128),
            rows(BLK, 48, 128),
            rows(5, 128, 128),
            rows(TWO, 4, 64, 128),
            rows(TWO, 128, 128),
            rows(TWO, 4, 32, 128),
            rows(TWO, 4, 24, 128),
            rows(BLK, 2, 80, 128),
            rows(BLK + 2, 2, 64, 128),
            rows(QUAD, 4, 48, 128),
            rows(32 * PITCH, 128),
            rows(TWO, 128, 128),
            rows(16 * PITCH, 128),
            *pair(HALF, 8),
            rows(HALF, 16, 128),
            *pair(2, HALF, 1),
            *pair(BLK, 2, 1),
            *pair(BLK, 2),
            rows(Z, 16, 128),
            rows(16 * STRIPS, 8, 128),
            rows(STRIPS, 152, 128),
            rows(STRIPS, 80, 128),
            rows(STRIPS, 80, 128),
            rows(16 * STRIPS, 8, 128),
            rows(16 * STRIPS, 8, 128),
            *pair(2, QUAD, 4, 1),
            *pair(2, TWO, 4, 1),
            *pair(TWO, 4, 2),
            pltpu.SemaphoreType.DMA((2 * len(CHUNKS) + 1,)),
            pltpu.SemaphoreType.DMA((copies,)),
            pltpu.SemaphoreType.DMA((copies,)),
        ],
        compiler_params=pltpu.CompilerParams(
            collective_id=0, has_side_effects=True, vmem_limit_bytes=51 * 2**20
        ),
    )(vorticity)
    o1, o2, o3 = pl.pallas_call(
        write_out,
        out_shape=results,
        in_specs=[pl.BlockSpec(memory_space=pl.ANY)] * 3,
        out_specs=[pl.BlockSpec(memory_space=pl.ANY)] * 3,
        scratch_shapes=[pltpu.SemaphoreType.DMA((3,))],
        compiler_params=pltpu.CompilerParams(vmem_limit_bytes=2**20),
    )(*inner)
    return o1, jnp.transpose(o2, (2, 0, 1)), jnp.transpose(o3, (2, 0, 1))


def solution(mesh):
    placed = P(None, "gx", "gy")
    return jax.shard_map(
        shards, mesh=mesh, in_specs=(placed,), out_specs=(placed,) * 3, check_vma=False
    )
```
